256 devices in a mesh: grp: 8 (over z_hi, y), dev: 32 (over z_lo, x, core).
Axes of the slice: x: 4, y: 4, z: 8 (z_hi: 2, z_lo: 4; z = z_hi * 4 + z_lo), core: 2. Of those that a mesh axis runs over, the one named last changes fastest.
Arguments:
- series: float32 [2, 1024, 32768], P(None, None, ('grp', 'dev')), may hold values from -6 to 6
- templates: float32 [200, 128], replicated, may hold values from -0.5 to 0.5
- drift_template: int32 [16], replicated, may hold values from 0 to 199
- drift_reach: int32 [16], replicated, may hold values from 4 to 32, as said below
Outputs:
- powers: float32 [16, 33554432], P(None, ('grp', 'dev'))
The draws below stay inside these ranges and needn't reach their ends.
Inputs may be any that keep to these rules, and one draw needn't show every extreme that they name: Drift d uses the taps t with 32 - drift_reach[d] <= t < 32 + drift_reach[d]; some drift uses all 64 taps.
All inputs are finite; a program needn't handle non-finite values.
Results may differ from the reference program's by a relative error of at most 0.000078.
Values sent between devices are 32-bit elements; how exact they have to be, the bound alone decides.
A program may use at most 64 MiB of HBM per device.

```python
import math
import jax
import jax.numpy as jnp
from jax import lax

P1 = 32
P2 = 32
Q1 = 128
Q2 = 256
P_SIZE = 1024
Q = 32768
TAPS = 64
TEMPLATES = 200
DRIFTS = 16


def draw_drift_reach(key, part):
    draw_key, spot_key = jax.random.split(jax.random.fold_in(key, 11))
    values = jax.random.randint(draw_key, (DRIFTS,), 4, TAPS // 2 + 1)
    chosen = jax.random.randint(spot_key, (), 0, DRIFTS)
    return jnp.where(jnp.arange(DRIFTS) == chosen, TAPS // 2, values).astype(jnp.int32)


def with_ends(entries, own_key, smallest, largest):
    shape = entries.shape
    spot = [jax.random.randint(jax.random.fold_in(own_key, axis), (), 0, shape[axis]) for axis in range(len(shape))]
    entries = entries.at[tuple(spot)].set(smallest)
    longest = shape.index(max(shape))
    spot[longest] = (spot[longest] + 1) % shape[longest]
    return entries.at[tuple(spot)].set(largest)


def levels(rng, shape, pieces, smallest, top_value):
    def one(position, blocks):
        draws = jax.random.uniform(jax.random.fold_in(jax.random.fold_in(rng, 6), position), (blocks,), jnp.float32, smallest / len(pieces), top_value / len(pieces))
        return jnp.repeat(jnp.exp(draws), shape[position] // blocks).reshape((-1,) + (1,) * (len(shape) - position - 1))

    factor_of = one(*pieces[0])
    for cut in pieces[1:]:
        factor_of = factor_of * one(*cut)
    return factor_of


def gaussian(stream_key, dims, width, reach, cuts=(), kind=jnp.bfloat16):
    drawn = jax.random.normal(stream_key, dims, jnp.float32) * width
    if len(cuts) > 0:
        drawn = levels(stream_key, dims, cuts, -0.22, 0.18) * drawn
    return jnp.clip(drawn, min=-reach, max=reach).astype(kind)


def setup_inputs(seed: int = 0) -> dict:
    keys = jax.random.split(jax.random.key(seed), 5)
    series = gaussian(keys[0], (2, P_SIZE, Q), 1.0, 6.0, ((2, 256),), jnp.float32)
    templates = gaussian(keys[1], (TEMPLATES, 2 * TAPS), (2 * TAPS) ** -0.5, 0.5, (), jnp.float32)
    drift_template = with_ends(jax.random.randint(keys[2], (DRIFTS,), 0, TEMPLATES), jax.random.fold_in(keys[2], 1), 0, TEMPLATES - 1).astype(jnp.int32)
    drift_reach = draw_drift_reach(jax.random.fold_in(keys[4], 71), 0)
    return {"series": series, "templates": templates, "drift_template": drift_template, "drift_reach": drift_reach}


def tap_kernels(templates, drift_template, drift_reach):
    chosen = templates[drift_template]
    taps_index = jnp.arange(TAPS, dtype=jnp.int32)[None, :]
    center = TAPS // 2
    inside = ((taps_index >= center - drift_reach[:, None]) & (taps_index < center + drift_reach[:, None])).astype(templates.dtype)
    return (chosen[:, :TAPS] * inside, chosen[:, TAPS:] * inside)

def banded(kernel_rows, window_width):
    lane_width = 128
    drift_count = kernel_rows.shape[0]
    padded = jnp.concatenate([kernel_rows, jnp.zeros((drift_count, window_width + 1 - TAPS), kernel_rows.dtype)], axis=1)
    tiled_rows = jnp.tile(padded, (1, lane_width))[:, :lane_width * window_width]
    return jnp.swapaxes(tiled_rows.reshape(drift_count, lane_width, window_width), 1, 2)

def reference(series, templates, drift_template, drift_reach):
    sample_count = 2 * P1 * P2 * Q1 * Q2
    samples = jnp.transpose(series, (1, 2, 0)).reshape(sample_count)
    bin_count = sample_count // 2
    spectrum = jnp.fft.rfft(samples)[:bin_count] / math.sqrt(sample_count)
    half_taps = TAPS // 2
    lane_width = 128
    window_width = lane_width + TAPS
    row_count = bin_count // lane_width
    extended = jnp.stack([jnp.pad(jnp.real(spectrum), (half_taps, half_taps)), jnp.pad(jnp.imag(spectrum), (half_taps, half_taps))])
    head_rows = extended[:, :bin_count].reshape(2, row_count, lane_width)
    rest_bins = jnp.concatenate([extended[:, lane_width:], jnp.zeros((2, lane_width - TAPS), extended.dtype)], axis=1)
    tail_rows = rest_bins.reshape(2, row_count, lane_width)[:, :, :TAPS]
    windows = jnp.concatenate([head_rows, tail_rows], axis=2)
    flat_windows = jnp.concatenate([windows[0], windows[1]], axis=1)
    kernel_real, kernel_imag = tap_kernels(templates, drift_template, drift_reach)
    band_real = banded(kernel_real, window_width)
    band_imag = banded(kernel_imag, window_width)
    matrices = jnp.concatenate([jnp.concatenate([band_real, band_imag], axis=2), jnp.concatenate([-band_imag, band_real], axis=2)], axis=1)

    def one_drift(matrix):
        response = jnp.dot(flat_windows, matrix, precision=lax.Precision.HIGHEST, preferred_element_type=jnp.float32)
        power_rows = response[:, :lane_width] * response[:, :lane_width] + response[:, lane_width:] * response[:, lane_width:]
        return power_rows.reshape(row_count * lane_width)
    return lax.map(one_drift, matrices)
```

```python
import math

import jax
import jax.numpy as jnp
from jax import lax
from jax.experimental import pallas as pl
from jax.experimental.pallas import tpu as pltpu
from jax.sharding import PartitionSpec as P

P1 = 32
P2 = 32
Q1 = 128
Q2 = 256
N = 67108864
M = 33554432
TAPS = 64


HIGHEST = lax.Precision.HIGHEST


def exchange_kernel(in_ref, out_ref, send_sem, recv_sem, own_sem):
    group_count = lax.axis_size("grp")
    member_count = lax.axis_size("dev")
    total = group_count * member_count
    me = lax.axis_index("grp") * member_count + lax.axis_index("dev")

    def place(target):
        return (target // member_count, lax.rem(target, member_count))

    barrier = pltpu.get_barrier_semaphore()

    def greet(step, carry):
        pl.semaphore_signal(
            barrier,
            inc=1,
            device_id=place(lax.rem(me + step, total)),
            device_id_type=pl.DeviceIdType.MESH,
        )
        return carry

    lax.fori_loop(1, total, greet, 0)
    pl.semaphore_wait(barrier, total - 1)

    def send(step, carry):
        target = lax.rem(me + step, total)
        pltpu.make_async_remote_copy(
            src_ref=in_ref.at[target],
            dst_ref=out_ref.at[me],
            send_sem=send_sem,
            recv_sem=recv_sem,
            device_id=place(target),
            device_id_type=pl.DeviceIdType.MESH,
        ).start()
        return carry

    lax.fori_loop(1, total, send, 0)
    own = pltpu.make_async_copy(in_ref.at[me], out_ref.at[me], own_sem)
    own.start()
    own.wait()
    others = pl.ds(0, total - 1)
    pltpu.make_async_copy(in_ref.at[others], out_ref.at[others], send_sem).wait()
    pltpu.make_async_copy(in_ref.at[others], out_ref.at[others], recv_sem).wait()


def exchange(parts, collective_id):
    shape = parts.shape
    parts = parts.reshape(shape[0], -1, 128)
    return pl.pallas_call(
        exchange_kernel,
        out_shape=jax.ShapeDtypeStruct(parts.shape, parts.dtype),
        in_specs=[pl.BlockSpec(memory_space=pltpu.VMEM)],
        out_specs=pl.BlockSpec(memory_space=pltpu.VMEM),
        scratch_shapes=[pltpu.SemaphoreType.DMA] * 3,
        compiler_params=pltpu.CompilerParams(
            collective_id=collective_id, has_side_effects=True, vmem_limit_bytes=16 << 20
        ),
    )(parts).reshape(shape)


def cut_along(value, dim, length):
    before, after = (value.shape[:dim], value.shape[dim + 1 :])
    return jnp.moveaxis(value.reshape(*before, length, -1, *after), dim, 0)


def in_order(parts, dim):
    shape = list(parts.shape[1:])
    shape[dim] *= parts.shape[0]
    return jnp.moveaxis(parts, 0, dim).reshape(shape)


def exchange_both(value, collective_id, axes, splits, concats):
    sizes = [lax.axis_size(a) for a in axes]
    parts = cut_along(value, splits[0], sizes[0])
    parts = jnp.moveaxis(cut_along(parts, splits[1] + 1, sizes[1]), 0, 1)
    inside = parts.shape[2:]
    parts = parts.reshape(-1, *inside)
    parts = exchange(parts, collective_id)
    parts = in_order(parts.reshape(*sizes, *inside), concats[0] + 1)
    return in_order(parts, concats[1])


def with_halo(value, sides, width):
    edges = {}
    for axis, dim in sides:
        size, length = (lax.axis_size(axis), value.shape[dim])
        up = [(i, (i + 1) % size) for i in range(size - 1)]
        last = lax.slice_in_dim(value, length - width, length, axis=dim)
        initial = lax.slice_in_dim(value, 0, width, axis=dim)
        edges[dim] = (
            lax.ppermute(last, axis, up),
            lax.ppermute(initial, axis, [(b, a) for a, b in up]),
        )
    done = []
    for _, dim in sides:
        low, high = edges[dim]
        around = [(width, width) if d in done else (0, 0) for d in range(value.ndim)]
        value = jnp.concatenate([jnp.pad(low, around), value, jnp.pad(high, around)], axis=dim)
        done.append(dim)
    return value


def dft_table(length):
    indices = jnp.arange(length, dtype=jnp.int32)
    product = indices[:, None] * indices[None, :] % length
    angles = product.astype(jnp.float32) * (-2.0 * math.pi / length)
    return (jnp.cos(angles), jnp.sin(angles))


def twiddle(row_index, col_index, length):
    product = row_index[:, None] * col_index[None, :] % length
    angles = product.astype(jnp.float32) * (-2.0 * math.pi / length)
    return (jnp.cos(angles), jnp.sin(angles))


def complex_einsum(formula, left_pair, right_pair):
    left_real, left_imag = left_pair
    right_real, right_imag = right_pair
    real_part = jnp.einsum(formula, left_real, right_real, precision=HIGHEST) - jnp.einsum(
        formula, left_imag, right_imag, precision=HIGHEST
    )
    imag_part = jnp.einsum(formula, left_real, right_imag, precision=HIGHEST) + jnp.einsum(
        formula, left_imag, right_real, precision=HIGHEST
    )
    return (real_part, imag_part)


def complex_scale(values, factor):
    values_real, values_imag = values
    factor_real, factor_imag = factor
    return (
        values_real * factor_real - values_imag * factor_imag,
        values_real * factor_imag + values_imag * factor_real,
    )


def column_transform(series):
    col_count = series.shape[2]
    blocks = series.reshape(2, P1, P2, col_count)
    first_table = dft_table(P1)
    sectioned = (
        jnp.einsum("ja,eabc->ejbc", first_table[0], blocks, precision=HIGHEST),
        jnp.einsum("ja,eabc->ejbc", first_table[1], blocks, precision=HIGHEST),
    )
    inner_turn = twiddle(jnp.arange(P1, dtype=jnp.int32), jnp.arange(P2, dtype=jnp.int32), P1 * P2)
    sectioned = complex_scale(
        sectioned, (inner_turn[0][None, :, :, None], inner_turn[1][None, :, :, None])
    )
    sectioned = complex_einsum("kb,ejbc->ekjc", dft_table(P2), sectioned)
    return (
        sectioned[0].reshape(2, P1 * P2, col_count),
        sectioned[1].reshape(2, P1 * P2, col_count),
    )


def row_transform(values):
    parts_count, row_count = (values[0].shape[0], values[0].shape[1])
    shaped = (
        values[0].reshape(parts_count, row_count, Q1, Q2),
        values[1].reshape(parts_count, row_count, Q1, Q2),
    )
    sectioned = complex_einsum("ja,kbac->kbjc", dft_table(Q1), shaped)
    inner_turn = twiddle(jnp.arange(Q1, dtype=jnp.int32), jnp.arange(Q2, dtype=jnp.int32), Q1 * Q2)
    sectioned = complex_scale(sectioned, (inner_turn[0][None, None], inner_turn[1][None, None]))
    sectioned = complex_einsum("lc,kbjc->kblj", dft_table(Q2), sectioned)
    return (
        sectioned[0].reshape(parts_count, row_count, Q1 * Q2),
        sectioned[1].reshape(parts_count, row_count, Q1 * Q2),
    )


def combine_halves(even_part, odd_part, frequency):
    angles = frequency.astype(jnp.float32) * (-2.0 * math.pi / N)
    turned = complex_scale(odd_part, (jnp.cos(angles), jnp.sin(angles)))
    norm_scale = 1.0 / math.sqrt(N)
    return ((even_part[0] + turned[0]) * norm_scale, (even_part[1] + turned[1]) * norm_scale)


def to_rows(stacked):
    group_count = lax.axis_size("grp")
    member_count = lax.axis_size("dev")
    leading = stacked.shape[0]
    col_count = stacked.shape[2]
    row_count = stacked.shape[1] // (group_count * member_count)
    shaped = stacked.reshape(leading, group_count, member_count, row_count, 1, 1, col_count)
    arrived = exchange_both(shaped, 0, ("grp", "dev"), (1, 2), (4, 5))
    return arrived.reshape(leading, row_count, group_count * member_count * col_count)


def to_segments(stacked):
    group_count = lax.axis_size("grp")
    member_count = lax.axis_size("dev")
    leading = stacked.shape[0]
    row_count = stacked.shape[1]
    col_count = stacked.shape[2] // (group_count * member_count)
    shaped = stacked.reshape(leading, 1, 1, row_count, group_count, member_count, col_count)
    arrived = exchange_both(shaped, 1, ("grp", "dev"), (4, 5), (1, 2))
    gathered = arrived.reshape(leading, group_count * member_count * row_count, col_count)
    return jnp.swapaxes(gathered, 1, 2).reshape(
        leading, col_count * group_count * member_count * row_count
    )


def tap_kernels(templates, drift_template, drift_reach):
    template_count = templates.shape[0]
    selector = (
        drift_template[:, None] == jnp.arange(template_count, dtype=jnp.int32)[None, :]
    ).astype(jnp.float32)
    chosen = jnp.dot(selector, templates, precision=HIGHEST, preferred_element_type=jnp.float32)
    taps_index = jnp.arange(TAPS, dtype=jnp.int32)[None, :]
    center = TAPS // 2
    inside = (
        (taps_index >= center - drift_reach[:, None]) & (taps_index < center + drift_reach[:, None])
    ).astype(jnp.float32)
    return (chosen[:, :TAPS] * inside, chosen[:, TAPS:] * inside)


def banded(kernel_rows, window_width):
    lane_width = 128
    drift_count = kernel_rows.shape[0]
    padded = jnp.concatenate(
        [kernel_rows, jnp.zeros((drift_count, window_width + 1 - TAPS), jnp.float32)], axis=1
    )
    tiled_rows = jnp.tile(padded, (1, lane_width))[:, : lane_width * window_width]
    return jnp.swapaxes(tiled_rows.reshape(drift_count, lane_width, window_width), 1, 2)


def correlate(extended, kernels, segment_bins):
    lane_width = 128
    row_count = segment_bins // lane_width
    window_width = lane_width + TAPS
    head_rows = extended[:, :segment_bins].reshape(2, row_count, lane_width)
    rest_bins = jnp.concatenate(
        [extended[:, lane_width:], jnp.zeros((2, lane_width - TAPS), jnp.float32)], axis=1
    )
    tail_rows = rest_bins.reshape(2, row_count, lane_width)[:, :, :TAPS]
    windows = jnp.concatenate([head_rows, tail_rows], axis=2)
    flat_windows = jnp.concatenate([windows[0], windows[1]], axis=1)
    band_real = banded(kernels[0], window_width)
    band_imag = banded(kernels[1], window_width)
    matrices = jnp.concatenate(
        [
            jnp.concatenate([band_real, band_imag], axis=2),
            jnp.concatenate([-band_imag, band_real], axis=2),
        ],
        axis=1,
    )
    response = jnp.einsum(
        "rw,dwo->dro", flat_windows, matrices, precision=HIGHEST, preferred_element_type=jnp.float32
    )
    power_rows = (
        response[:, :, :lane_width] * response[:, :, :lane_width]
        + response[:, :, lane_width:] * response[:, :, lane_width:]
    )
    return power_rows.reshape(power_rows.shape[0], row_count * lane_width)


def local(series, templates, drift_template, drift_reach):
    position = lax.axis_index(("grp", "dev"))
    col_count = series.shape[2]
    row_total = P1 * P2
    row_frequency = jnp.arange(row_total, dtype=jnp.int32)
    columns = position * col_count + jnp.arange(col_count, dtype=jnp.int32)
    column_turn = twiddle(row_frequency, columns, M)
    section_real, section_imag = column_transform(series)
    turned = complex_scale(
        (section_real, section_imag), (column_turn[0][None], column_turn[1][None])
    )
    by_rows = to_rows(jnp.concatenate([turned[0], turned[1]], axis=0))
    spectrum = row_transform((by_rows[0:2], by_rows[2:4]))
    row_count = by_rows.shape[1]
    row_index = position * row_count + jnp.arange(row_count, dtype=jnp.int32)
    frequency = row_index[:, None] + row_total * jnp.arange(Q1 * Q2, dtype=jnp.int32)[None, :]
    whole_real, whole_imag = combine_halves(
        (spectrum[0][0], spectrum[1][0]), (spectrum[0][1], spectrum[1][1]), frequency
    )
    segment = to_segments(jnp.stack([whole_real, whole_imag]))
    segment_bins = segment.shape[1]
    kernels = tap_kernels(templates, drift_template, drift_reach)
    extended = with_halo(segment, ((("grp", "dev"), 1),), TAPS // 2)
    return correlate(extended, kernels, segment_bins)


def solution(mesh):
    return jax.shard_map(
        local,
        mesh=mesh,
        in_specs=(P(None, None, ("grp", "dev")), P(), P(), P()),
        out_specs=P(None, ("grp", "dev")),
        check_vma=False,
    )
```

```python
import functools
import math

import jax
import jax.numpy as jnp
import ml_dtypes
import numpy as np
from jax import lax
from jax.experimental import pallas as pl
from jax.experimental.pallas import tpu as pltpu
from jax.sharding import PartitionSpec as P

N = 67108864
ROWS = 1024
HALF = 256
LANES = 128
TAPS = 64
DRIFTS = 16
DEVICES = 256
MEMBERS = 32
F32 = jnp.float32
BF16 = jnp.bfloat16
MESH = pl.DeviceIdType.MESH


def root(product, length):
    angles = (np.asarray(product, np.int64) % length) * (-2.0 * math.pi / length)
    return np.cos(angles), np.sin(angles)


def halves(table):
    table = np.asarray(table, np.float32)
    high = table.astype(ml_dtypes.bfloat16)
    low = (table - high.astype(np.float32)).astype(ml_dtypes.bfloat16)
    return high, low


@functools.cache
def tables():
    index = np.arange
    done = {}
    cos, sin = root(index(512)[:, None] * index(ROWS)[None, :], ROWS)
    sin[0] = 1.0 - 2.0 * (index(ROWS) % 2)
    column = np.stack([cos, sin]).reshape(2, 2, HALF, ROWS).transpose(1, 0, 2, 3)
    done["column"] = halves(column.reshape(2, 512, ROWS))
    sample = 2 * index(LANES)[None, :] + index(2)[:, None]
    turn = root(sample[:, None, :] * index(512)[None, :, None], N)
    done["turn"] = (np.stack(turn, axis=1) / math.sqrt(N)).astype(np.float32)
    phase = root(2 * LANES * index(DEVICES)[:, None] * index(512)[None, :], N)
    done["phase"] = np.stack(phase, axis=1).reshape(DEVICES, 8, LANES).astype(np.float32)
    middle = root(512 * (2 * LANES * index(HALF)[None, :, None] + sample[:, None, :]), N)
    done["middle"] = np.stack(middle, axis=1).astype(np.float32)
    cos, sin = root(index(HALF)[:, None] * index(HALF)[None, :], HALF)
    done["outer"] = halves(np.block([[cos, -sin], [sin, cos]]))
    twist = root(index(HALF)[:, None] * index(LANES)[None, :], HALF * LANES)
    done["twist"] = np.stack(twist).astype(np.float32)
    cos, sin = root(index(LANES)[:, None] * index(LANES)[None, :], LANES)
    back = slice(None, None, -1)
    done["inner"] = halves(np.block([[cos, -sin], [sin, cos], [cos[back], -sin[back]], [sin[back], cos[back]]]))
    join = np.stack(root(index(HALF)[None, :] + HALF * index(LANES)[:, None], 2 * HALF * LANES))
    done["join"] = np.concatenate([join, join[:, back]]).astype(np.float32)
    order = np.zeros((512, 512), np.float32)
    for row in range(512):
        source = 512 - row
        order[row, source if row else 0] = 1.0
    done["order"] = order.astype(ml_dtypes.bfloat16)
    edge = np.zeros((64, 64), np.float32)
    for row in range(64):
        edge[row, row // 32 * 32 + 31 - row % 32] = 1.0
    done["edge"] = edge.astype(ml_dtypes.bfloat16)
    done["mirror"] = np.eye(LANES, dtype=np.float32)[back].astype(ml_dtypes.bfloat16)
    return done


def split(value):
    high = value.astype(BF16)
    return high, (value - high.astype(F32)).astype(BF16)


def product(left, right):
    dot = functools.partial(jnp.dot, preferred_element_type=F32)
    return dot(left[0], right[0]) + (dot(left[0], right[1]) + dot(left[1], right[0]))


def product_t(left, right):
    def dot(a, b):
        return lax.dot_general(a, b, (((1,), (1,)), ((), ())), preferred_element_type=F32)

    return dot(left[0], right[0]) + (dot(left[0], right[1]) + dot(left[1], right[0]))


def place(target):
    return (target // MEMBERS, lax.rem(target, MEMBERS))


def spectrum_kernel(
    series_in, column_hi_in, column_lo_in, turn_in, phase_in, middle_in, outer_hi_in, outer_lo_in,
    twist_in, inner_hi_in, inner_lo_in, join_in, templates, chosen, reach,
    bins, halo, bands,
    series, column_hi, column_lo, turn, phase, middle, outer_hi, outer_lo, twist, inner_hi, inner_lo, join,
    send_one, recv_one, send_two, edge_out, edge_in,
    load_sem, own_sem, send_sem, recv_sem, edge_send_sem, edge_recv_sem,
):
    me = lax.axis_index("grp") * MEMBERS + lax.axis_index("dev")
    pairs = [
        (series_in, series), (column_hi_in, column_hi), (column_lo_in, column_lo), (turn_in, turn),
        (phase_in.at[me], phase), (middle_in, middle), (outer_hi_in, outer_hi), (outer_lo_in, outer_lo),
        (twist_in, twist), (inner_hi_in, inner_hi), (inner_lo_in, inner_lo), (join_in, join),
    ]
    loads = [pltpu.make_async_copy(a, b, load_sem.at[i]) for i, (a, b) in enumerate(pairs)]
    for load in loads:
        load.start()

    barrier = pltpu.get_barrier_semaphore()

    def greet(step, carry):
        target = place(lax.rem(me + step, DEVICES))
        pl.semaphore_signal(barrier, inc=1, device_id=target, device_id_type=MESH)
        return carry

    lax.fori_loop(1, DEVICES, greet, 0, unroll=5)
    for load in loads:
        load.wait()

    high, low = split(jnp.concatenate([series[0], series[1]], axis=1))
    padded = jnp.concatenate([phase[...]] * 16, axis=0)
    phase_columns = jnp.transpose(padded)

    def column_part(chunk):
        def rows(part):
            at = pl.ds(part * HALF, HALF)
            return product((column_hi[chunk, at, :], column_lo[chunk, at, :]), (high, low))

        real, imag = rows(0), rows(1)
        blocks = (2 * chunk, 2 * chunk + 1)
        phase_real = jnp.concatenate([phase_columns[:, b : b + 1] for b in blocks], axis=0)
        phase_imag = jnp.concatenate([phase_columns[:, b + 4 : b + 5] for b in blocks], axis=0)
        for e in range(2):
            turn_real = turn[e, 0, pl.ds(chunk * HALF, HALF), :]
            turn_imag = turn[e, 1, pl.ds(chunk * HALF, HALF), :]
            full_real = turn_real * phase_real - turn_imag * phase_imag
            full_imag = turn_real * phase_imag + turn_imag * phase_real
            a, b = real[:, e * LANES : (e + 1) * LANES], imag[:, e * LANES : (e + 1) * LANES]
            send_one[chunk, pl.ds(2 * e, HALF, stride=4), :] = a * full_real - b * full_imag
            send_one[chunk, pl.ds(2 * e + 1, HALF, stride=4), :] = a * full_imag + b * full_real

    def send_all(source, target_ref, chunk, number):
        mine = pl.ds(pl.multiple_of(4 * me, 4), 4)
        own = pltpu.make_async_copy(source.at[chunk, mine], target_ref.at[chunk, mine], own_sem.at[number])
        own.start()

        def send(step, carry):
            target = lax.rem(me + step, DEVICES)
            pltpu.make_async_remote_copy(
                src_ref=source.at[chunk, pl.ds(pl.multiple_of(4 * target, 4), 4)],
                dst_ref=target_ref.at[chunk, mine],
                send_sem=send_sem.at[number],
                recv_sem=recv_sem.at[number],
                device_id=place(target),
                device_id_type=MESH,
            ).start()
            return carry

        lax.fori_loop(1, DEVICES, send, 0, unroll=5)
        own.wait()

    def wait_all(source, target_ref, chunk, sem):
        others = pl.ds(0, 4 * (DEVICES - 1))
        pltpu.make_async_copy(source.at[chunk, others], target_ref.at[chunk, others], sem).wait()

    column_part(0)
    pl.semaphore_wait(barrier, DEVICES - 1)
    send_all(send_one, recv_one, 0, 0)
    column_part(1)
    send_all(send_one, recv_one, 1, 1)

    lane = lax.broadcasted_iota(jnp.int32, (1, LANES), 1)
    for d in range(DRIFTS):
        taps = templates[pl.ds(chosen[d], 1), :]
        tap = lax.rem(lane, TAPS)
        inside = (tap >= TAPS // 2 - reach[d]) & (tap < TAPS // 2 + reach[d])
        taps = jnp.where(inside, taps, 0.0)
        real = jnp.where(lane < TAPS, taps, 0.0)
        imag = jnp.where(lane < TAPS, pltpu.roll(taps, TAPS, 1), 0.0)
        band_real = pltpu.roll(jnp.broadcast_to(real, (TAPS, LANES)), 0, 1, stride=1, stride_axis=0)
        band_imag = pltpu.roll(jnp.broadcast_to(imag, (TAPS, LANES)), 0, 1, stride=1, stride_axis=0)
        for part, wide in enumerate(([band_real, -band_imag], [band_imag, band_real])):
            for level, value in enumerate(split(jnp.concatenate(wide, axis=1))):
                bands[level, d // 2, pl.ds(part * LANES + d % 2 * TAPS, TAPS), :] = value

    def row_part(real, imag):
        wide = product((outer_hi[...], outer_lo[...]), split(jnp.concatenate([real, imag], axis=0)))
        done = []
        for e in range(2):
            a, b = wide[:HALF, e * LANES : (e + 1) * LANES], wide[HALF:, e * LANES : (e + 1) * LANES]
            turned = [a * twist[0] - b * twist[1], a * twist[1] + b * twist[0]]
            done.append(
                product_t((inner_hi[...], inner_lo[...]), split(jnp.concatenate(turned, axis=1)))
            )
        return done

    def store(chunk, part, value, flip):
        for h in range(2):
            first = 4 * (1 - h if flip else h) + part
            send_two[chunk, pl.ds(first, LANES, stride=8), :] = value[:, h * LANES : (h + 1) * LANES]

    def store_direct(chunk, even, odd):
        odd_real, odd_imag = odd[0:128], odd[128:256]
        store(chunk, 0, even[0:128] + (join[0] * odd_real - join[1] * odd_imag), False)
        store(chunk, 1, even[128:256] + (join[0] * odd_imag + join[1] * odd_real), False)

    def store_mirrored(chunk, even, odd):
        odd_real, odd_imag = odd[256:384], odd[384:512]
        store(chunk, 2, even[256:384] - (join[2] * odd_real - join[3] * odd_imag), True)
        store(chunk, 3, (join[2] * odd_imag + join[3] * odd_real) - even[384:512], True)

    def arrived(chunk):
        return [recv_one[chunk, pl.ds(s, HALF, stride=4), :] for s in range(4)]

    def rows_of(chunk):
        parts = arrived(chunk)
        real = jnp.concatenate([parts[0], parts[2]], axis=1)
        imag = jnp.concatenate([parts[1], parts[3]], axis=1)
        if chunk == 0:
            imag = imag * (me != 0).astype(F32)
        even, odd = row_part(real, imag)
        store_direct(chunk, even, odd)
        store_mirrored(chunk, even, odd)

    wait_all(send_one, recv_one, 0, recv_sem.at[0])
    rows_of(0)

    @pl.when(me == 0)
    def _():
        parts = arrived(0)
        real = jnp.concatenate([parts[1] * middle[0, 0], parts[3] * middle[1, 0]], axis=1)
        imag = jnp.concatenate([parts[1] * middle[0, 1], parts[3] * middle[1, 1]], axis=1)
        even, odd = row_part(real, imag)
        store_mirrored(0, even, odd)

    send_all(send_two, bins, 0, 2)
    wait_all(send_one, recv_one, 1, recv_sem.at[1])
    rows_of(1)
    send_all(send_two, bins, 1, 3)
    wait_all(send_two, bins, 0, recv_sem.at[2])

    def edge_rows(side):
        first = (4 + 2, 0)[side]
        return jnp.concatenate([bins[0, pl.ds(first + part, 32, stride=4), :] for part in range(2)], axis=0)

    last = DEVICES - 1
    near = [lax.rem(me + 1, DEVICES), lax.rem(me + last, DEVICES)]
    sends = [me < last, me > 0]
    gets = [me > 0, me < last]
    copies = []
    for side in range(2):
        edge_out[side] = edge_rows(side)
        edge_in[side] = jnp.zeros((64, LANES), F32)
    for side in range(2):
        copy = pltpu.make_async_remote_copy(
            src_ref=edge_out.at[side],
            dst_ref=edge_in.at[2 + side],
            send_sem=edge_send_sem.at[side],
            recv_sem=edge_recv_sem.at[side],
            device_id=place(near[side]),
            device_id_type=MESH,
        )
        pl.when(sends[side])(copy.start)
        copies.append(copy)
    first_lane = lax.broadcasted_iota(jnp.int32, (64, LANES), 1) == 0
    for side in range(2):
        pl.when(gets[side])(copies[side].wait_recv)

        @pl.when(gets[side])
        def _():
            edge_in[side] = edge_in[2 + side]

        halo[side] = pltpu.roll(jnp.where(first_lane, edge_in[side], edge_out[side]), LANES - 1, 1)
        pl.when(sends[side])(copies[side].wait_send)

    wait_all(send_two, bins, 1, recv_sem.at[3])
    for number, source, target_ref in ((0, send_one, recv_one), (1, send_one, recv_one), (2, send_two, bins), (3, send_two, bins)):
        wait_all(source, target_ref, number % 2, send_sem.at[number])


def correlate_kernel(bins, halo, order, edge, mirror, bands, out, rows):
    step = pl.program_id(0)

    @pl.when(step == 0)
    def _():
        def flip(value):
            return jnp.dot(value.astype(BF16), mirror[...], preferred_element_type=F32).astype(BF16)

        for part in range(2):
            direct = jnp.concatenate([bins[c, pl.ds(part, HALF, stride=4), :] for c in range(2)], axis=0)
            for level, value in enumerate(split(direct)):
                rows[2 * level + part, pl.ds(32, 512), :] = value
            for level, value in enumerate(split(halo[1, pl.ds(32 * part, 32), :])):
                rows[2 * level + part, pl.ds(1056, 32), :] = value
            mirrored = jnp.concatenate([bins[c, pl.ds(2 + part, HALF, stride=4), :] for c in range(2)], axis=0)
            moved = jnp.dot(order[...], jnp.concatenate(split(mirrored), axis=1), preferred_element_type=F32)
            for level in range(2):
                rows[2 * level + part, pl.ds(544, 512), :] = flip(moved[:, level * LANES : (level + 1) * LANES])
        moved = jnp.dot(edge[...], jnp.concatenate(split(halo[0]), axis=1), preferred_element_type=F32)
        for level in range(2):
            flipped = flip(moved[:, level * LANES : (level + 1) * LANES])
            for part in range(2):
                rows[2 * level + part, pl.ds(0, 32), :] = flipped[32 * part : 32 * part + 32]

    def window(level, odd):
        at = pl.ds(pl.multiple_of(step * LANES + odd * TAPS, TAPS), LANES)
        return jnp.concatenate([jnp.transpose(rows[2 * level + part, at, :]) for part in range(2)], axis=1)

    windows = [jnp.concatenate([window(level, odd) for odd in range(2)], axis=0) for level in range(2)]
    flat = out.reshape(2 * LANES * 8, LANES)
    low_lanes = lax.broadcasted_iota(jnp.int32, (LANES, LANES), 1) < TAPS
    for pair in range(DRIFTS // 2):
        response = product_t(windows, (bands[0, pair], bands[1, pair]))
        real, imag = response[:, :LANES], response[:, LANES:]
        power = real * real + imag * imag
        even, odd = power[:LANES], power[LANES:]
        first = jnp.where(low_lanes, even, pltpu.roll(odd, TAPS, 1))
        second = jnp.where(low_lanes, pltpu.roll(even, TAPS, 1), odd)
        for d, value in ((2 * pair, first), (2 * pair + 1, second)):
            flat[pl.ds(d // 8 * 1024 + d % 8, LANES, stride=8), :] = value


def spectrum(series, templates, drift_template, drift_reach):
    made = tables()
    inputs = [series, *made["column"], made["turn"], made["phase"], made["middle"], *made["outer"], made["twist"], *made["inner"], made["join"]]
    inputs = [jnp.asarray(value) for value in inputs]
    shapes = [value.shape for value in inputs]
    shapes[4] = (8, LANES)
    copies = [pltpu.VMEM(shape, value.dtype) for shape, value in zip(shapes, inputs)]
    chunked = pltpu.VMEM((2, 4 * DEVICES, LANES), F32)
    far = pl.BlockSpec(memory_space=pltpu.HBM)
    vmem = pl.BlockSpec(memory_space=pltpu.VMEM)
    smem = pl.BlockSpec(memory_space=pltpu.SMEM)
    dma = pltpu.SemaphoreType.DMA
    return pl.pallas_call(
        spectrum_kernel,
        name="spectrum",
        out_shape=(
            jax.ShapeDtypeStruct((2, 4 * DEVICES, LANES), F32),
            jax.ShapeDtypeStruct((2, 64, LANES), F32),
            jax.ShapeDtypeStruct((2, DRIFTS // 2, 256, 256), BF16),
        ),
        in_specs=[far] * len(inputs) + [vmem, smem, smem],
        out_specs=(vmem, vmem, vmem),
        scratch_shapes=[
            *copies, chunked, chunked, chunked,
            pltpu.VMEM((2, 64, LANES), F32), pltpu.VMEM((4, 64, LANES), F32),
            dma((len(inputs),)), dma((4,)), dma((4,)), dma((4,)), dma((2,)), dma((2,)),
        ],
        compiler_params=pltpu.CompilerParams(
            collective_id=0, has_side_effects=True, vmem_limit_bytes=60 << 20
        ),
    )(*inputs, templates, drift_template, drift_reach)


def correlate(bins, halo, bands):
    made = tables()
    shifts = [jnp.asarray(made[name]) for name in ("order", "edge", "mirror")]
    vmem = pl.BlockSpec(memory_space=pltpu.VMEM)
    powers = pl.pallas_call(
        correlate_kernel,
        name="correlate",
        grid=(8,),
        out_shape=jax.ShapeDtypeStruct((2, LANES, 8, 8, LANES), F32),
        in_specs=[vmem] * 6,
        out_specs=pl.BlockSpec((2, LANES, 1, 8, LANES), lambda h: (0, 0, h, 0, 0)),
        scratch_shapes=[pltpu.VMEM((4, 1088, LANES), BF16)],
        compiler_params=pltpu.CompilerParams(vmem_limit_bytes=32 << 20),
    )(bins, halo, *shifts, bands)
    return powers.transpose(0, 3, 1, 2, 4).reshape(DRIFTS, LANES * ROWS)


def local(series, templates, drift_template, drift_reach):
    bins, halo, bands = spectrum(series, templates, drift_template, drift_reach)
    return correlate(bins, halo, bands)


def solution(mesh):
    return jax.shard_map(
        local,
        mesh=mesh,
        in_specs=(P(None, None, ("grp", "dev")), P(), P(), P()),
        out_specs=P(None, ("grp", "dev")),
        check_vma=False,
    )
```

```python
import functools
import math

import jax
import jax.numpy as jnp
import ml_dtypes
import numpy as np
from jax import lax
from jax.experimental import pallas as pl
from jax.experimental.pallas import tpu as pltpu
from jax.sharding import PartitionSpec as P

N = 67108864
ROWS = 1024
HALF = 256
LANES = 128
TAPS = 64
DRIFTS = 16
DEVICES = 256
MEMBERS = 32
GROUPS = 8
MIDDLE = 832
F32 = jnp.float32
BF16 = jnp.bfloat16
MESH = pl.DeviceIdType.MESH


def root(product, length):
    angles = (np.asarray(product, np.int64) % length) * (-2.0 * math.pi / length)
    return np.cos(angles), np.sin(angles)


def halves(table):
    table = np.asarray(table, np.float32)
    high = table.astype(ml_dtypes.bfloat16)
    low = (table - high.astype(np.float32)).astype(ml_dtypes.bfloat16)
    return high, low


@functools.cache
def tables():
    index = np.arange
    done = {}
    cos, sin = root(index(512)[:, None] * index(ROWS)[None, :], ROWS)
    sin[0] = 1.0 - 2.0 * (index(ROWS) % 2)
    column = np.stack([cos, sin]).reshape(2, 2, HALF, ROWS).transpose(1, 0, 2, 3)
    done["column"] = halves(column.reshape(2, 512, ROWS))
    sample = 2 * index(LANES)[None, :] + index(2)[:, None]
    turn = root(sample[:, None, :] * index(512)[None, :, None], N)
    done["turn"] = (np.stack(turn, axis=1) / math.sqrt(N)).astype(np.float32)
    phase = root(2 * LANES * index(DEVICES)[:, None] * index(512)[None, :], N)
    done["phase"] = np.stack(phase, axis=1).reshape(DEVICES, 8, LANES).astype(np.float32)
    middle = root(512 * (2 * LANES * index(HALF)[None, :, None] + sample[:, None, :]), N)
    done["middle"] = np.stack(middle, axis=1).astype(np.float32)
    cos, sin = root(index(HALF)[:, None] * index(HALF)[None, :], HALF)
    done["outer"] = halves(np.block([[cos, -sin], [sin, cos]]))
    twist = root(index(HALF)[:, None] * index(LANES)[None, :], HALF * LANES)
    done["twist"] = np.stack(twist).astype(np.float32)
    cos, sin = root(index(LANES)[:, None] * index(LANES)[None, :], LANES)
    back = slice(None, None, -1)
    done["inner"] = halves(np.block([[cos, -sin], [sin, cos], [cos[back], -sin[back]], [sin[back], cos[back]]]))
    join = np.stack(root(index(HALF)[None, :] + HALF * index(LANES)[:, None], 2 * HALF * LANES))
    done["join"] = np.concatenate([join, join[:, back]]).astype(np.float32)
    order = np.zeros((512, 512), np.float32)
    for row in range(512):
        source = 512 - row
        order[row, source if row else 0] = 1.0
    done["order"] = order.astype(ml_dtypes.bfloat16)
    edge = np.zeros((64, 64), np.float32)
    for row in range(64):
        edge[row, row // 32 * 32 + 31 - row % 32] = 1.0
    done["edge"] = edge.astype(ml_dtypes.bfloat16)
    done["mirror"] = np.eye(LANES, dtype=np.float32)[back].astype(ml_dtypes.bfloat16)
    return done


def split(value):
    high = value.astype(BF16)
    return high, (value - high.astype(F32)).astype(BF16)


def product(left, right):
    dot = functools.partial(jnp.dot, preferred_element_type=F32)
    return dot(left[0], right[0]) + (dot(left[0], right[1]) + dot(left[1], right[0]))


def product_t(left, right):
    def dot(a, b):
        return lax.dot_general(a, b, (((1,), (1,)), ((), ())), preferred_element_type=F32)

    return dot(left[0], right[0]) + (dot(left[0], right[1]) + dot(left[1], right[0]))


def place(target):
    return (target // MEMBERS, lax.rem(target, MEMBERS))


def spectrum_kernel(
    series_in, column_hi_in, column_lo_in, turn_in, phase_in, middle_in, outer_hi_in, outer_lo_in,
    twist_in, inner_hi_in, inner_lo_in, join_in, order_in, edge_in, mirror_in, templates, chosen, reach,
    rows_out, early_out, bands_out,
    series, column_hi, column_lo, turn, phase, middle, outer_hi, outer_lo, twist, inner_hi, inner_lo, join,
    order, edge, mirror,
    send_one, recv_one, send_two, bins, halo_out, halo_in, rows, mixed, early, bands,
    load_sem, own_sem, send_sem, recv_sem, halo_send_sem, halo_recv_sem, out_sem, ready,
):
    me = lax.axis_index("grp") * MEMBERS + lax.axis_index("dev")
    pairs = [
        (series_in, series), (column_hi_in, column_hi), (column_lo_in, column_lo), (turn_in, turn),
        (phase_in.at[me], phase), (middle_in, middle), (outer_hi_in, outer_hi), (outer_lo_in, outer_lo),
        (twist_in, twist), (inner_hi_in, inner_hi), (inner_lo_in, inner_lo), (join_in, join),
        (order_in, order), (edge_in, edge), (mirror_in, mirror),
    ]
    loads = [pltpu.make_async_copy(a, b, load_sem.at[i]) for i, (a, b) in enumerate(pairs)]
    def tell(semaphore, size, target):
        def one(step, carry):
            pl.semaphore_signal(semaphore, inc=1, device_id=target(step), device_id_type=MESH)
            return carry

        lax.fori_loop(1, size, one, 0)

    barrier = pltpu.get_barrier_semaphore()
    group, member = lax.axis_index("grp"), lax.axis_index("dev")
    tell(barrier, GROUPS, lambda step: (lax.rem(group + step, GROUPS), member))
    tell(barrier, MEMBERS, lambda step: (group, lax.rem(member + step, MEMBERS)))
    for load in loads:
        load.start()
    pl.semaphore_wait(barrier, GROUPS + MEMBERS - 2)
    tell(ready, MEMBERS, lambda step: (group, lax.rem(member + step, MEMBERS)))
    for load in loads:
        load.wait()

    high, low = split(jnp.concatenate([series[0], series[1]], axis=1))
    padded = jnp.concatenate([phase[...]] * 16, axis=0)
    phase_columns = jnp.transpose(padded)

    def column_part(chunk):
        def rows(part):
            at = pl.ds(part * HALF, HALF)
            return product((column_hi[chunk, at, :], column_lo[chunk, at, :]), (high, low))

        real, imag = rows(0), rows(1)
        blocks = (2 * chunk, 2 * chunk + 1)
        phase_real = jnp.concatenate([phase_columns[:, b : b + 1] for b in blocks], axis=0)
        phase_imag = jnp.concatenate([phase_columns[:, b + 4 : b + 5] for b in blocks], axis=0)
        for e in range(2):
            turn_real = turn[e, 0, pl.ds(chunk * HALF, HALF), :]
            turn_imag = turn[e, 1, pl.ds(chunk * HALF, HALF), :]
            full_real = turn_real * phase_real - turn_imag * phase_imag
            full_imag = turn_real * phase_imag + turn_imag * phase_real
            a, b = real[:, e * LANES : (e + 1) * LANES], imag[:, e * LANES : (e + 1) * LANES]
            send_one[chunk, pl.ds(2 * e, HALF, stride=4), :] = a * full_real - b * full_imag
            send_one[chunk, pl.ds(2 * e + 1, HALF, stride=4), :] = a * full_imag + b * full_real

    def send_all(source, target_ref, chunk, number):
        mine = pl.ds(pl.multiple_of(4 * me, 4), 4)
        own = pltpu.make_async_copy(source.at[chunk, mine], target_ref.at[chunk, mine], own_sem.at[number])
        own.start()

        def send(step, carry):
            target = lax.rem(me + step, DEVICES)
            pltpu.make_async_remote_copy(
                src_ref=source.at[chunk, pl.ds(pl.multiple_of(4 * target, 4), 4)],
                dst_ref=target_ref.at[chunk, mine],
                send_sem=send_sem.at[number],
                recv_sem=recv_sem.at[number],
                device_id=place(target),
                device_id_type=MESH,
            ).start()
            return carry

        lax.fori_loop(1, DEVICES, send, 0, unroll=5)
        own.wait()

    def wait_all(source, target_ref, chunk, sem):
        others = pl.ds(0, 4 * (DEVICES - 1))
        pltpu.make_async_copy(source.at[chunk, others], target_ref.at[chunk, others], sem).wait()

    column_part(0)
    pl.semaphore_wait(ready, MEMBERS - 1)
    send_all(send_one, recv_one, 0, 0)
    column_part(1)
    send_all(send_one, recv_one, 1, 1)

    lane = lax.broadcasted_iota(jnp.int32, (1, LANES), 1)
    for d in range(DRIFTS):
        taps = templates[pl.ds(chosen[d], 1), :]
        tap = lax.rem(lane, TAPS)
        inside = (tap >= TAPS // 2 - reach[d]) & (tap < TAPS // 2 + reach[d])
        taps = jnp.where(inside, taps, 0.0)
        real = jnp.where(lane < TAPS, taps, 0.0)
        imag = jnp.where(lane < TAPS, pltpu.roll(taps, TAPS, 1), 0.0)
        band_real = pltpu.roll(jnp.broadcast_to(real, (TAPS, LANES)), 0, 1, stride=1, stride_axis=0)
        band_imag = pltpu.roll(jnp.broadcast_to(imag, (TAPS, LANES)), 0, 1, stride=1, stride_axis=0)
        for part, wide in enumerate(([band_real, -band_imag], [band_imag, band_real])):
            for level, value in enumerate(split(jnp.concatenate(wide, axis=1))):
                bands[d // 2, level, pl.ds(part * LANES + d % 2 * TAPS, TAPS), :] = value

    bands_copy = pltpu.make_async_copy(bands, bands_out, out_sem.at[0])
    bands_copy.start()

    def row_part(real, imag):
        wide = product((outer_hi[...], outer_lo[...]), split(jnp.concatenate([real, imag], axis=0)))
        done = []
        for e in range(2):
            a, b = wide[:HALF, e * LANES : (e + 1) * LANES], wide[HALF:, e * LANES : (e + 1) * LANES]
            turned = [a * twist[0] - b * twist[1], a * twist[1] + b * twist[0]]
            done.append(
                product_t((inner_hi[...], inner_lo[...]), split(jnp.concatenate(turned, axis=1)))
            )
        return done

    def store(chunk, part, value, flip):
        for h in range(2):
            first = 4 * (1 - h if flip else h) + part
            send_two[chunk, pl.ds(first, LANES, stride=8), :] = value[:, h * LANES : (h + 1) * LANES]

    def store_direct(chunk, even, odd):
        odd_real, odd_imag = odd[0:128], odd[128:256]
        store(chunk, 0, even[0:128] + (join[0] * odd_real - join[1] * odd_imag), False)
        store(chunk, 1, even[128:256] + (join[0] * odd_imag + join[1] * odd_real), False)

    def store_mirrored(chunk, even, odd):
        odd_real, odd_imag = odd[256:384], odd[384:512]
        store(chunk, 2, even[256:384] - (join[2] * odd_real - join[3] * odd_imag), True)
        store(chunk, 3, (join[2] * odd_imag + join[3] * odd_real) - even[384:512], True)

    def arrived(chunk):
        return [recv_one[chunk, pl.ds(s, HALF, stride=4), :] for s in range(4)]

    def rows_of(chunk):
        parts = arrived(chunk)
        real = jnp.concatenate([parts[0], parts[2]], axis=1)
        imag = jnp.concatenate([parts[1], parts[3]], axis=1)
        if chunk == 0:
            imag = imag * (me != 0).astype(F32)
        even, odd = row_part(real, imag)
        store_direct(chunk, even, odd)
        store_mirrored(chunk, even, odd)

    wait_all(send_one, recv_one, 0, recv_sem.at[0])
    rows_of(0)

    @pl.when(me == 0)
    def _():
        parts = arrived(0)
        real = jnp.concatenate([parts[1] * middle[0, 0], parts[3] * middle[1, 0]], axis=1)
        imag = jnp.concatenate([parts[1] * middle[0, 1], parts[3] * middle[1, 1]], axis=1)
        even, odd = row_part(real, imag)
        store_mirrored(0, even, odd)

    send_all(send_two, bins, 0, 2)
    wait_all(send_one, recv_one, 1, recv_sem.at[1])
    rows_of(1)
    send_all(send_two, bins, 1, 3)
    wait_all(send_two, bins, 0, recv_sem.at[2])

    def halo_rows(side):
        first = (4 + 2, 0)[side]
        return jnp.concatenate([bins[0, pl.ds(first + part, 32, stride=4), :] for part in range(2)], axis=0)

    last = DEVICES - 1
    near = [lax.rem(me + 1, DEVICES), lax.rem(me + last, DEVICES)]
    sends = [me < last, me > 0]
    gets = [me > 0, me < last]
    copies = []
    for side in range(2):
        halo_out[side] = halo_rows(side)
        halo_in[side] = jnp.zeros((64, LANES), F32)
    for side in range(2):
        copy = pltpu.make_async_remote_copy(
            src_ref=halo_out.at[side],
            dst_ref=halo_in.at[2 + side],
            send_sem=halo_send_sem.at[side],
            recv_sem=halo_recv_sem.at[side],
            device_id=place(near[side]),
            device_id_type=MESH,
        )
        pl.when(sends[side])(copy.start)
        copies.append(copy)

    def flip(value):
        return jnp.dot(value.astype(BF16), mirror[...], preferred_element_type=F32).astype(BF16)

    def put_direct(chunk):
        for part in range(2):
            for level, value in enumerate(split(bins[chunk, pl.ds(part, HALF, stride=4), :])):
                rows[2 * level + part, pl.ds(32 + HALF * chunk, HALF), :] = value
            wide = jnp.concatenate(split(bins[chunk, pl.ds(2 + part, HALF, stride=4), :]), axis=1)
            mixed[pl.ds(HALF * chunk, HALF), pl.ds(2 * LANES * part, 2 * LANES)] = wide

    def put_mirrored(moved, first, count):
        for part in range(2):
            for level in range(2):
                at = (2 * part + level) * LANES
                rows[2 * level + part, pl.ds(first, count), :] = flip(moved[:, at : at + LANES])

    put_direct(0)
    moved = jnp.dot(order[pl.ds(HALF, HALF), pl.ds(0, HALF)], mixed[pl.ds(0, HALF), :], preferred_element_type=F32)
    put_mirrored(moved, 800, HALF)

    first_lane = lax.broadcasted_iota(jnp.int32, (64, LANES), 1) == 0
    sides = []
    for side in range(2):
        pl.when(gets[side])(copies[side].wait_recv)

        @pl.when(gets[side])
        def _():
            halo_in[side] = halo_in[2 + side]

        sides.append(split(pltpu.roll(jnp.where(first_lane, halo_in[side], halo_out[side]), LANES - 1, 1)))
        pl.when(sends[side])(copies[side].wait_send)
    moved = jnp.dot(edge[...], jnp.concatenate(sides[0], axis=1), preferred_element_type=F32)
    for level in range(2):
        flipped = flip(moved[:, level * LANES : (level + 1) * LANES])
        for part in range(2):
            rows[2 * level + part, pl.ds(0, 32), :] = flipped[32 * part : 32 * part + 32]
            rows[2 * level + part, pl.ds(1056, 32), :] = sides[1][level][32 * part : 32 * part + 32]

    correlate_tiles(rows, bands, [0, 14 * TAPS], early.reshape(2 * LANES * 2 * 8, LANES), lambda pair: None)
    early_copy = pltpu.make_async_copy(early, early_out, out_sem.at[1])
    early_copy.start()

    wait_all(send_two, bins, 1, recv_sem.at[3])
    put_direct(1)
    moved = jnp.dot(order[pl.ds(0, 272), :], mixed[...], preferred_element_type=F32)
    put_mirrored(moved, 544, 272)
    rows_copy = pltpu.make_async_copy(rows.at[:, pl.ds(LANES, MIDDLE)], rows_out, out_sem.at[2])
    rows_copy.start()
    for number, source, target_ref in (
        (0, send_one, recv_one), (1, send_one, recv_one), (2, send_two, bins), (3, send_two, bins)
    ):
        wait_all(source, target_ref, number % 2, send_sem.at[number])
    bands_copy.wait()
    early_copy.wait()
    rows_copy.wait()


def correlate_tiles(rows, bands, starts, flat, before):
    def window(level, first):
        at = pl.ds(first, LANES)
        return jnp.concatenate([jnp.transpose(rows[2 * level + part, at, :]) for part in range(2)], axis=1)

    count = len(starts)
    firsts = [start + odd * TAPS for start in starts for odd in range(2)]
    windows = [jnp.concatenate([window(level, first) for first in firsts], axis=0) for level in range(2)]
    low_lanes = lax.broadcasted_iota(jnp.int32, (LANES, LANES), 1) < TAPS
    for pair in range(DRIFTS // 2):
        before(pair)
        response = product_t(windows, (bands[pair, 0], bands[pair, 1]))
        real, imag = response[:, :LANES], response[:, LANES:]
        power = real * real + imag * imag
        for tile in range(count):
            even = power[2 * LANES * tile : 2 * LANES * tile + LANES]
            odd = power[2 * LANES * tile + LANES : 2 * LANES * (tile + 1)]
            first = jnp.where(low_lanes, even, pltpu.roll(odd, TAPS, 1))
            second = jnp.where(low_lanes, pltpu.roll(even, TAPS, 1), odd)
            for d, value in ((2 * pair, first), (2 * pair + 1, second)):
                at = (d // 8 * LANES * count + tile) * 8 + d % 8
                flat[pl.ds(at, LANES, stride=8 * count), :] = value


def correlate_kernel(rows_in, early_in, bands_in, out, rows, bands, *rest):
    tiles, (row_sem, band_sem, early_sem, out_sem) = rest[:6], rest[6:]
    row_copy = pltpu.make_async_copy(rows_in, rows, row_sem)
    row_copy.start()
    band_copies = []
    for pair in range(DRIFTS // 2):
        copy = pltpu.make_async_copy(bands_in.at[pair], bands.at[pair], band_sem.at[pair])
        copy.start()
        band_copies.append(copy)
    copies = []
    for slot, tile in enumerate((0, 7)):
        copy = pltpu.make_async_copy(early_in.at[:, :, slot], out.at[:, :, tile], early_sem.at[slot])
        copy.start()
        copies.append(copy)
    row_copy.wait()
    for tile in range(1, 7):
        held = tiles[tile - 1]

        def before(pair):
            if tile == 1:
                band_copies[pair].wait()

        correlate_tiles(rows, bands, [(tile - 1) * LANES], held.reshape(2 * LANES * 8, LANES), before)
        copy = pltpu.make_async_copy(held, out.at[:, :, tile], out_sem.at[tile - 1])
        copy.start()
        copies.append(copy)
    for copy in copies:
        copy.wait()


def spectrum(series, templates, drift_template, drift_reach):
    made = tables()
    inputs = [
        series, *made["column"], made["turn"], made["phase"], made["middle"], *made["outer"],
        made["twist"], *made["inner"], made["join"], made["order"], made["edge"], made["mirror"],
    ]
    inputs = [jnp.asarray(value) for value in inputs]
    shapes = [value.shape for value in inputs]
    shapes[4] = (8, LANES)
    copies = [pltpu.VMEM(shape, value.dtype) for shape, value in zip(shapes, inputs)]
    chunked = pltpu.VMEM((2, 4 * DEVICES, LANES), F32)
    far = pl.BlockSpec(memory_space=pl.ANY)
    smem = pl.BlockSpec(memory_space=pltpu.SMEM)
    dma = pltpu.SemaphoreType.DMA
    early = (2, LANES, 2, 8, LANES)
    bands = (DRIFTS // 2, 2, 256, 256)
    return pl.pallas_call(
        spectrum_kernel,
        name="spectrum",
        out_shape=(
            jax.ShapeDtypeStruct((4, MIDDLE, LANES), BF16),
            jax.ShapeDtypeStruct(early, F32),
            jax.ShapeDtypeStruct(bands, BF16),
        ),
        in_specs=[far] * len(inputs) + [pl.BlockSpec(memory_space=pltpu.VMEM), smem, smem],
        out_specs=(far, far, far),
        scratch_shapes=[
            *copies, chunked, chunked, chunked, chunked,
            pltpu.VMEM((2, 64, LANES), F32), pltpu.VMEM((4, 64, LANES), F32),
            pltpu.VMEM((4, 1088, LANES), BF16), pltpu.VMEM((512, 512), BF16),
            pltpu.VMEM(early, F32), pltpu.VMEM(bands, BF16),
            dma((len(inputs),)), dma((4,)), dma((4,)), dma((4,)), dma((2,)), dma((2,)), dma((3,)),
            pltpu.SemaphoreType.REGULAR,
        ],
        compiler_params=pltpu.CompilerParams(
            collective_id=0, has_side_effects=True, vmem_limit_bytes=60 << 20
        ),
    )(*inputs, templates, drift_template, drift_reach)


def correlate(rows, early, bands):
    far = pl.BlockSpec(memory_space=pl.ANY)
    dma = pltpu.SemaphoreType.DMA
    powers = pl.pallas_call(
        correlate_kernel,
        name="correlate",
        out_shape=jax.ShapeDtypeStruct((2, LANES, 8, 8, LANES), F32),
        in_specs=[far] * 3,
        out_specs=far,
        scratch_shapes=[
            pltpu.VMEM(rows.shape, BF16), pltpu.VMEM(bands.shape, BF16),
            *[pltpu.VMEM((2, LANES, 8, LANES), F32) for _ in range(6)],
            dma, dma((DRIFTS // 2,)), dma((2,)), dma((6,)),
        ],
        compiler_params=pltpu.CompilerParams(vmem_limit_bytes=60 << 20),
    )(rows, early, bands)
    return powers.transpose(0, 3, 1, 2, 4).reshape(DRIFTS, LANES * ROWS)


def local(series, templates, drift_template, drift_reach):
    return correlate(*spectrum(series, templates, drift_template, drift_reach))


def solution(mesh):
    return jax.shard_map(
        local,
        mesh=mesh,
        in_specs=(P(None, None, ("grp", "dev")), P(), P(), P()),
        out_specs=P(None, ("grp", "dev")),
        check_vma=False,
    )
```

```python
import functools
import math

import jax
import jax.numpy as jnp
import ml_dtypes
import numpy as np
from jax import lax
from jax.experimental import pallas as pl
from jax.experimental.pallas import tpu as pltpu
from jax.sharding import PartitionSpec as P

N = 67108864
ROWS = 1024
HALF = 256
LANES = 128
TAPS = 64
DRIFTS = 16
DEVICES = 256
MEMBERS = 32
GROUPS = 8
EXTENDED = 1088
F32 = jnp.float32
BF16 = jnp.bfloat16
MESH = pl.DeviceIdType.MESH


def root(product, length):
    angles = (np.asarray(product, np.int64) % length) * (-2.0 * math.pi / length)
    return np.cos(angles), np.sin(angles)


def halves(table):
    table = np.asarray(table, np.float32)
    high = table.astype(ml_dtypes.bfloat16)
    low = (table - high.astype(np.float32)).astype(ml_dtypes.bfloat16)
    return high, low


@functools.cache
def tables():
    index = np.arange
    done = {}
    cos, sin = root(index(512)[:, None] * index(ROWS)[None, :], ROWS)
    sin[0] = 1.0 - 2.0 * (index(ROWS) % 2)
    column = np.stack([cos, sin]).reshape(2, 2, HALF, ROWS).transpose(1, 0, 2, 3)
    done["column"] = halves(column.reshape(2, 512, ROWS))
    sample = 2 * index(LANES)[None, :] + index(2)[:, None]
    turn = root(sample[:, None, :] * index(512)[None, :, None], N)
    done["turn"] = (np.stack(turn, axis=1) / math.sqrt(N)).astype(np.float32)
    phase = root(2 * LANES * index(DEVICES)[:, None] * index(512)[None, :], N)
    done["phase"] = np.stack(phase, axis=1).reshape(DEVICES, 8, LANES).astype(np.float32)
    middle = root(512 * (2 * LANES * index(HALF)[None, :, None] + sample[:, None, :]), N)
    done["middle"] = np.stack(middle, axis=1).astype(np.float32)
    cos, sin = root(index(HALF)[:, None] * index(HALF)[None, :], HALF)
    done["outer"] = halves(np.block([[cos, -sin], [sin, cos]]))
    twist = root(index(HALF)[:, None] * index(LANES)[None, :], HALF * LANES)
    done["twist"] = np.stack(twist).astype(np.float32)
    cos, sin = root(index(LANES)[:, None] * index(LANES)[None, :], LANES)
    back = slice(None, None, -1)
    done["inner"] = halves(np.block([[cos, -sin], [sin, cos], [cos[back], -sin[back]], [sin[back], cos[back]]]))
    join = np.stack(root(index(HALF)[None, :] + HALF * index(LANES)[:, None], 2 * HALF * LANES))
    done["join"] = np.concatenate([join, join[:, back]]).astype(np.float32)
    order = np.zeros((512, 512), np.float32)
    for row in range(512):
        source = 512 - row
        order[row, source if row else 0] = 1.0
    done["order"] = order.astype(ml_dtypes.bfloat16)
    edge = np.zeros((64, 64), np.float32)
    for row in range(64):
        edge[row, row // 32 * 32 + 31 - row % 32] = 1.0
    done["edge"] = edge.astype(ml_dtypes.bfloat16)
    done["mirror"] = np.eye(LANES, dtype=np.float32)[back].astype(ml_dtypes.bfloat16)
    return done


def split(value):
    high = value.astype(BF16)
    return high, (value - high.astype(F32)).astype(BF16)


def product(left, right):
    dot = functools.partial(jnp.dot, preferred_element_type=F32)
    return dot(left[0], right[0]) + (dot(left[0], right[1]) + dot(left[1], right[0]))


def product_t(left, right):
    def dot(a, b):
        return lax.dot_general(a, b, (((1,), (1,)), ((), ())), preferred_element_type=F32)

    return dot(left[0], right[0]) + (dot(left[0], right[1]) + dot(left[1], right[0]))


def place(target):
    return (target // MEMBERS, lax.rem(target, MEMBERS))


def spectrum_kernel(
    series_in, column_hi_in, column_lo_in, turn_in, phase_in, middle_in, outer_hi_in, outer_lo_in,
    twist_in, inner_hi_in, inner_lo_in, join_in, order_in, edge_in, mirror_in, templates, chosen, reach,
    rows_out, bands_out,
    series, column_hi, column_lo, turn, phase, middle, outer_hi, outer_lo, twist, inner_hi, inner_lo, join,
    order, edge, mirror,
    send_one, recv_one, send_two, bins, halo_out, halo_in, rows, mixed, bands,
    load_sem, own_sem, send_sem, recv_sem, halo_send_sem, halo_recv_sem, out_sem, ready,
):
    me = lax.axis_index("grp") * MEMBERS + lax.axis_index("dev")
    pairs = [
        (phase_in.at[me], phase), (series_in, series),
        (column_hi_in.at[0], column_hi.at[0]), (column_lo_in.at[0], column_lo.at[0]), (turn_in, turn),
        (column_hi_in.at[1], column_hi.at[1]), (column_lo_in.at[1], column_lo.at[1]), (middle_in, middle), (outer_hi_in, outer_hi), (outer_lo_in, outer_lo),
        (twist_in, twist), (inner_hi_in, inner_hi), (inner_lo_in, inner_lo), (join_in, join),
        (order_in, order), (edge_in, edge), (mirror_in, mirror),
    ]
    loads = [pltpu.make_async_copy(a, b, load_sem.at[i]) for i, (a, b) in enumerate(pairs)]
    def tell(semaphore, size, target):
        def one(step, carry):
            pl.semaphore_signal(semaphore, inc=1, device_id=target(step), device_id_type=MESH)
            return carry

        lax.fori_loop(1, size, one, 0)

    for load in loads[:5]:
        load.start()
    barrier = pltpu.get_barrier_semaphore()
    group, member = lax.axis_index("grp"), lax.axis_index("dev")
    tell(barrier, GROUPS, lambda step: (lax.rem(group + step, GROUPS), member))
    tell(barrier, MEMBERS, lambda step: (group, lax.rem(member + step, MEMBERS)))
    pl.semaphore_wait(barrier, GROUPS + MEMBERS - 2)
    tell(ready, MEMBERS, lambda step: (group, lax.rem(member + step, MEMBERS)))
    for load in loads[5:]:
        load.start()
    for load in loads[:5]:
        load.wait()

    high, low = split(jnp.concatenate([series[0], series[1]], axis=1))
    padded = jnp.concatenate([phase[...]] * 16, axis=0)
    phase_columns = jnp.transpose(padded)

    def column_part(chunk):
        def rows(part):
            at = pl.ds(part * HALF, HALF)
            return product((column_hi[chunk, at, :], column_lo[chunk, at, :]), (high, low))

        real, imag = rows(0), rows(1)
        blocks = (2 * chunk, 2 * chunk + 1)
        phase_real = jnp.concatenate([phase_columns[:, b : b + 1] for b in blocks], axis=0)
        phase_imag = jnp.concatenate([phase_columns[:, b + 4 : b + 5] for b in blocks], axis=0)
        for e in range(2):
            turn_real = turn[e, 0, pl.ds(chunk * HALF, HALF), :]
            turn_imag = turn[e, 1, pl.ds(chunk * HALF, HALF), :]
            full_real = turn_real * phase_real - turn_imag * phase_imag
            full_imag = turn_real * phase_imag + turn_imag * phase_real
            a, b = real[:, e * LANES : (e + 1) * LANES], imag[:, e * LANES : (e + 1) * LANES]
            send_one[chunk, pl.ds(2 * e, HALF, stride=4), :] = a * full_real - b * full_imag
            send_one[chunk, pl.ds(2 * e + 1, HALF, stride=4), :] = a * full_imag + b * full_real

    def send_all(source, target_ref, chunk, number):
        mine = pl.ds(pl.multiple_of(4 * me, 4), 4)
        own = pltpu.make_async_copy(source.at[chunk, mine], target_ref.at[chunk, mine], own_sem.at[number])
        own.start()

        def send(step, carry):
            target = lax.rem(me + step, DEVICES)
            pltpu.make_async_remote_copy(
                src_ref=source.at[chunk, pl.ds(pl.multiple_of(4 * target, 4), 4)],
                dst_ref=target_ref.at[chunk, mine],
                send_sem=send_sem.at[number],
                recv_sem=recv_sem.at[number],
                device_id=place(target),
                device_id_type=MESH,
            ).start()
            return carry

        lax.fori_loop(1, DEVICES, send, 0, unroll=5)
        own.wait()

    def wait_all(source, target_ref, chunk, sem):
        others = pl.ds(0, 4 * (DEVICES - 1))
        pltpu.make_async_copy(source.at[chunk, others], target_ref.at[chunk, others], sem).wait()

    column_part(0)
    pl.semaphore_wait(ready, MEMBERS - 1)
    send_all(send_one, recv_one, 0, 0)
    for load in loads[5:]:
        load.wait()
    column_part(1)
    send_all(send_one, recv_one, 1, 1)

    lane = lax.broadcasted_iota(jnp.int32, (1, LANES), 1)
    for d in range(DRIFTS):
        taps = templates[pl.ds(chosen[d], 1), :]
        tap = lax.rem(lane, TAPS)
        inside = (tap >= TAPS // 2 - reach[d]) & (tap < TAPS // 2 + reach[d])
        taps = jnp.where(inside, taps, 0.0)
        real = jnp.where(lane < TAPS, taps, 0.0)
        imag = jnp.where(lane < TAPS, pltpu.roll(taps, TAPS, 1), 0.0)
        band_real = pltpu.roll(jnp.broadcast_to(real, (TAPS, LANES)), 0, 1, stride=1, stride_axis=0)
        band_imag = pltpu.roll(jnp.broadcast_to(imag, (TAPS, LANES)), 0, 1, stride=1, stride_axis=0)
        for part, wide in enumerate(([band_real, -band_imag], [band_imag, band_real])):
            for level, value in enumerate(split(jnp.concatenate(wide, axis=1))):
                bands[d // 2, level, pl.ds(part * LANES + d % 2 * TAPS, TAPS), :] = value

    bands_copy = pltpu.make_async_copy(bands, bands_out, out_sem.at[0])
    bands_copy.start()

    def row_part(real, imag):
        wide = product((outer_hi[...], outer_lo[...]), split(jnp.concatenate([real, imag], axis=0)))
        done = []
        for e in range(2):
            a, b = wide[:HALF, e * LANES : (e + 1) * LANES], wide[HALF:, e * LANES : (e + 1) * LANES]
            turned = [a * twist[0] - b * twist[1], a * twist[1] + b * twist[0]]
            done.append(
                product_t((inner_hi[...], inner_lo[...]), split(jnp.concatenate(turned, axis=1)))
            )
        return done

    def store(chunk, part, value, flip):
        for h in range(2):
            first = 4 * (1 - h if flip else h) + part
            send_two[chunk, pl.ds(first, LANES, stride=8), :] = value[:, h * LANES : (h + 1) * LANES]

    def store_direct(chunk, even, odd):
        odd_real, odd_imag = odd[0:128], odd[128:256]
        store(chunk, 0, even[0:128] + (join[0] * odd_real - join[1] * odd_imag), False)
        store(chunk, 1, even[128:256] + (join[0] * odd_imag + join[1] * odd_real), False)

    def store_mirrored(chunk, even, odd):
        odd_real, odd_imag = odd[256:384], odd[384:512]
        store(chunk, 2, even[256:384] - (join[2] * odd_real - join[3] * odd_imag), True)
        store(chunk, 3, (join[2] * odd_imag + join[3] * odd_real) - even[384:512], True)

    def arrived(chunk):
        return [recv_one[chunk, pl.ds(s, HALF, stride=4), :] for s in range(4)]

    def rows_of(chunk):
        parts = arrived(chunk)
        real = jnp.concatenate([parts[0], parts[2]], axis=1)
        imag = jnp.concatenate([parts[1], parts[3]], axis=1)
        if chunk == 0:
            imag = imag * (me != 0).astype(F32)
        even, odd = row_part(real, imag)
        store_direct(chunk, even, odd)
        store_mirrored(chunk, even, odd)

    wait_all(send_one, recv_one, 0, recv_sem.at[0])
    rows_of(0)

    @pl.when(me == 0)
    def _():
        parts = arrived(0)
        real = jnp.concatenate([parts[1] * middle[0, 0], parts[3] * middle[1, 0]], axis=1)
        imag = jnp.concatenate([parts[1] * middle[0, 1], parts[3] * middle[1, 1]], axis=1)
        even, odd = row_part(real, imag)
        store_mirrored(0, even, odd)

    send_all(send_two, bins, 0, 2)
    wait_all(send_one, recv_one, 1, recv_sem.at[1])
    rows_of(1)
    send_all(send_two, bins, 1, 3)
    wait_all(send_two, bins, 0, recv_sem.at[2])

    def halo_rows(side):
        first = (4 + 2, 0)[side]
        return jnp.concatenate([bins[0, pl.ds(first + part, 32, stride=4), :] for part in range(2)], axis=0)

    last = DEVICES - 1
    near = [lax.rem(me + 1, DEVICES), lax.rem(me + last, DEVICES)]
    sends = [me < last, me > 0]
    gets = [me > 0, me < last]
    copies = []
    for side in range(2):
        halo_out[side] = halo_rows(side)
        halo_in[side] = jnp.zeros((64, LANES), F32)
    for side in range(2):
        copy = pltpu.make_async_remote_copy(
            src_ref=halo_out.at[side],
            dst_ref=halo_in.at[2 + side],
            send_sem=halo_send_sem.at[side],
            recv_sem=halo_recv_sem.at[side],
            device_id=place(near[side]),
            device_id_type=MESH,
        )
        pl.when(sends[side])(copy.start)
        copies.append(copy)

    def flip(value):
        return jnp.dot(value.astype(BF16), mirror[...], preferred_element_type=F32).astype(BF16)

    def put_direct(chunk):
        for part in range(2):
            for level, value in enumerate(split(bins[chunk, pl.ds(part, HALF, stride=4), :])):
                rows[2 * level + part, pl.ds(32 + HALF * chunk, HALF), :] = value
            wide = jnp.concatenate(split(bins[chunk, pl.ds(2 + part, HALF, stride=4), :]), axis=1)
            mixed[pl.ds(HALF * chunk, HALF), pl.ds(2 * LANES * part, 2 * LANES)] = wide

    def put_mirrored(moved, first, count):
        for part in range(2):
            for level in range(2):
                at = (2 * part + level) * LANES
                rows[2 * level + part, pl.ds(first, count), :] = flip(moved[:, at : at + LANES])

    put_direct(0)
    moved = jnp.dot(order[pl.ds(HALF, HALF), pl.ds(0, HALF)], mixed[pl.ds(0, HALF), :], preferred_element_type=F32)
    put_mirrored(moved, 800, HALF)

    first_lane = lax.broadcasted_iota(jnp.int32, (64, LANES), 1) == 0
    sides = []
    for side in range(2):
        pl.when(gets[side])(copies[side].wait_recv)

        @pl.when(gets[side])
        def _():
            halo_in[side] = halo_in[2 + side]

        sides.append(split(pltpu.roll(jnp.where(first_lane, halo_in[side], halo_out[side]), LANES - 1, 1)))
        pl.when(sends[side])(copies[side].wait_send)
    moved = jnp.dot(edge[...], jnp.concatenate(sides[0], axis=1), preferred_element_type=F32)
    for level in range(2):
        flipped = flip(moved[:, level * LANES : (level + 1) * LANES])
        for part in range(2):
            rows[2 * level + part, pl.ds(0, 32), :] = flipped[32 * part : 32 * part + 32]
            rows[2 * level + part, pl.ds(1056, 32), :] = sides[1][level][32 * part : 32 * part + 32]

    def rows_part(number, first, count):
        at = pl.ds(first, count)
        copy = pltpu.make_async_copy(rows.at[:, at], rows_out.at[:, at], out_sem.at[number])
        copy.start()
        return copy

    rows_copies = [rows_part(1, 0, 288), rows_part(2, 816, 272)]
    wait_all(send_two, bins, 1, recv_sem.at[3])
    put_direct(1)
    moved = jnp.dot(order[pl.ds(0, 272), :], mixed[...], preferred_element_type=F32)
    put_mirrored(moved, 544, 272)
    rows_copies.append(rows_part(3, 288, 528))
    for number, source, target_ref in (
        (0, send_one, recv_one), (1, send_one, recv_one), (2, send_two, bins), (3, send_two, bins)
    ):
        wait_all(source, target_ref, number % 2, send_sem.at[number])
    for copy in (bands_copy, *rows_copies):
        copy.wait()


def correlate_kernel(rows_in, bands_in, out, rows, bands, *rest):
    tiles, (row_sem, band_sem, out_sem) = rest[:8], rest[8:]
    row_copy = pltpu.make_async_copy(rows_in, rows, row_sem)
    row_copy.start()
    band_copies = []
    for pair in range(DRIFTS // 2):
        copy = pltpu.make_async_copy(bands_in.at[pair], bands.at[pair], band_sem.at[pair])
        copy.start()
        band_copies.append(copy)

    def windows_of(tile):
        def window(level, odd):
            at = pl.ds(tile * LANES + odd * TAPS, LANES)
            return jnp.concatenate([jnp.transpose(rows[2 * level + part, at, :]) for part in range(2)], axis=1)

        return [jnp.concatenate([window(level, odd) for odd in range(2)], axis=0) for level in range(2)]

    low_lanes = lax.broadcasted_iota(jnp.int32, (LANES, LANES), 1) < TAPS
    copies, pending = [], []
    row_copy.wait()
    for copy in band_copies:
        copy.wait()
    coming = windows_of(0)
    for tile in range(8):
        windows = coming
        if tile < 7:
            coming = windows_of(tile + 1)
        flat = tiles[tile].reshape(2 * LANES * 8, LANES)
        for pair in range(DRIFTS // 2):
            response = product_t(windows, (bands[pair, 0], bands[pair, 1]))
            real, imag = response[:, :LANES], response[:, LANES:]
            power = real * real + imag * imag
            even, odd = power[:LANES], power[LANES:]
            first = jnp.where(low_lanes, even, pltpu.roll(odd, TAPS, 1))
            second = jnp.where(low_lanes, pltpu.roll(even, TAPS, 1), odd)
            for d, value in ((2 * pair, first), (2 * pair + 1, second)):
                flat[pl.ds(d // 8 * LANES * 8 + d % 8, LANES, stride=8), :] = value
        pending.append(pltpu.make_async_copy(tiles[tile], out.at[:, :, tile], out_sem.at[tile]))
        if tile in (3, 6, 7):
            for copy in pending:
                copy.start()
            copies += pending
            pending = []
    for copy in copies:
        copy.wait()


def spectrum(series, templates, drift_template, drift_reach):
    made = tables()
    inputs = [
        series, *made["column"], made["turn"], made["phase"], made["middle"], *made["outer"],
        made["twist"], *made["inner"], made["join"], made["order"], made["edge"], made["mirror"],
    ]
    inputs = [jnp.asarray(value) for value in inputs]
    shapes = [value.shape for value in inputs]
    shapes[4] = (8, LANES)
    copies = [pltpu.VMEM(shape, value.dtype) for shape, value in zip(shapes, inputs)]
    chunked = pltpu.VMEM((2, 4 * DEVICES, LANES), F32)
    far = pl.BlockSpec(memory_space=pl.ANY)
    smem = pl.BlockSpec(memory_space=pltpu.SMEM)
    dma = pltpu.SemaphoreType.DMA
    bands = (DRIFTS // 2, 2, 256, 256)
    return pl.pallas_call(
        spectrum_kernel,
        name="spectrum",
        out_shape=(
            jax.ShapeDtypeStruct((4, EXTENDED, LANES), BF16),
            jax.ShapeDtypeStruct(bands, BF16),
        ),
        in_specs=[far] * len(inputs) + [pl.BlockSpec(memory_space=pltpu.VMEM), smem, smem],
        out_specs=(far, far),
        scratch_shapes=[
            *copies, chunked, chunked, chunked, chunked,
            pltpu.VMEM((2, 64, LANES), F32), pltpu.VMEM((4, 64, LANES), F32),
            pltpu.VMEM((4, EXTENDED, LANES), BF16), pltpu.VMEM((512, 512), BF16),
            pltpu.VMEM(bands, BF16),
            dma((len(inputs) + 2,)), dma((4,)), dma((4,)), dma((4,)), dma((2,)), dma((2,)), dma((4,)),
            pltpu.SemaphoreType.REGULAR,
        ],
        compiler_params=pltpu.CompilerParams(
            collective_id=0, has_side_effects=True, vmem_limit_bytes=60 << 20
        ),
    )(*inputs, templates, drift_template, drift_reach)


def correlate(rows, bands):
    far = pl.BlockSpec(memory_space=pl.ANY)
    dma = pltpu.SemaphoreType.DMA
    powers = pl.pallas_call(
        correlate_kernel,
        name="correlate",
        out_shape=jax.ShapeDtypeStruct((2, LANES, 8, 8, LANES), F32),
        in_specs=[far] * 2,
        out_specs=far,
        scratch_shapes=[
            pltpu.VMEM(rows.shape, BF16), pltpu.VMEM(bands.shape, BF16),
            *[pltpu.VMEM((2, LANES, 8, LANES), F32) for _ in range(8)],
            dma, dma((DRIFTS // 2,)), dma((8,)),
        ],
        compiler_params=pltpu.CompilerParams(vmem_limit_bytes=60 << 20),
    )(rows, bands)
    return powers.transpose(0, 3, 1, 2, 4).reshape(DRIFTS, LANES * ROWS)


def local(series, templates, drift_template, drift_reach):
    return correlate(*spectrum(series, templates, drift_template, drift_reach))


def solution(mesh):
    return jax.shard_map(
        local,
        mesh=mesh,
        in_specs=(P(None, None, ("grp", "dev")), P(), P(), P()),
        out_specs=P(None, ("grp", "dev")),
        check_vma=False,
    )
```

```python
import functools
import math

import jax
import jax.numpy as jnp
import ml_dtypes
import numpy as np
from jax import lax
from jax.experimental import pallas as pl
from jax.experimental.pallas import tpu as pltpu
from jax.sharding import PartitionSpec as P

N = 67108864
ROWS = 1024
HALF = 256
LANES = 128
TAPS = 64
DRIFTS = 16
DEVICES = 256
MEMBERS = 32
GROUPS = 8
EXTENDED = 1088
F32 = jnp.float32
BF16 = jnp.bfloat16
MESH = pl.DeviceIdType.MESH


def root(product, length):
    angles = (np.asarray(product, np.int64) % length) * (-2.0 * math.pi / length)
    return np.cos(angles), np.sin(angles)


def halves(table):
    table = np.asarray(table, np.float32)
    high = table.astype(ml_dtypes.bfloat16)
    low = (table - high.astype(np.float32)).astype(ml_dtypes.bfloat16)
    return high, low


@functools.cache
def tables():
    index = np.arange
    done = {}
    cos, sin = root(index(512)[:, None] * index(ROWS)[None, :], ROWS)
    sin[0] = 1.0 - 2.0 * (index(ROWS) % 2)
    column = np.stack([cos, sin]).reshape(2, 2, HALF, ROWS).transpose(1, 0, 2, 3)
    done["column"] = halves(column.reshape(2, 512, ROWS))
    sample = 2 * index(LANES)[None, :] + index(2)[:, None]
    turn = root(sample[:, None, :] * index(512)[None, :, None], N)
    done["turn"] = (np.stack(turn, axis=1) / math.sqrt(N)).astype(np.float32)
    phase = root(2 * LANES * index(DEVICES)[:, None] * index(512)[None, :], N)
    done["phase"] = np.stack(phase, axis=1).reshape(DEVICES, 8, LANES).astype(np.float32)
    middle = root(512 * (2 * LANES * index(HALF)[None, :, None] + sample[:, None, :]), N)
    done["middle"] = np.stack(middle, axis=1).astype(np.float32)
    cos, sin = root(index(HALF)[:, None] * index(HALF)[None, :], HALF)
    done["outer"] = halves(np.block([[cos, -sin], [sin, cos]]))
    twist = root(index(HALF)[:, None] * index(LANES)[None, :], HALF * LANES)
    done["twist"] = np.stack(twist).astype(np.float32)
    cos, sin = root(index(LANES)[:, None] * index(LANES)[None, :], LANES)
    back = slice(None, None, -1)
    done["inner"] = halves(np.block([[cos, -sin], [sin, cos], [cos[back], -sin[back]], [sin[back], cos[back]]]))
    join = np.stack(root(index(HALF)[None, :] + HALF * index(LANES)[:, None], 2 * HALF * LANES))
    done["join"] = np.concatenate([join, join[:, back]]).astype(np.float32)
    order = np.zeros((512, 512), np.float32)
    for row in range(512):
        source = 512 - row
        order[row, source if row else 0] = 1.0
    done["order"] = order.astype(ml_dtypes.bfloat16)
    edge = np.zeros((64, 64), np.float32)
    for row in range(64):
        edge[row, row // 32 * 32 + 31 - row % 32] = 1.0
    done["edge"] = edge.astype(ml_dtypes.bfloat16)
    done["mirror"] = np.eye(LANES, dtype=np.float32)[back].astype(ml_dtypes.bfloat16)
    return done


def split(value):
    high = value.astype(BF16)
    return high, (value - high.astype(F32)).astype(BF16)


def product(left, right):
    dot = functools.partial(jnp.dot, preferred_element_type=F32)
    return dot(left[0], right[0]) + (dot(left[0], right[1]) + dot(left[1], right[0]))


def product_t(left, right):
    def dot(a, b):
        return lax.dot_general(a, b, (((1,), (1,)), ((), ())), preferred_element_type=F32)

    return dot(left[0], right[0]) + (dot(left[0], right[1]) + dot(left[1], right[0]))


def place(target):
    return (target // MEMBERS, lax.rem(target, MEMBERS))


def spectrum_kernel(
    series_in, column_hi_in, column_lo_in, turn_in, phase_in, middle_in, outer_hi_in, outer_lo_in,
    twist_in, inner_hi_in, inner_lo_in, join_in, order_in, edge_in, mirror_in, templates, chosen, reach,
    rows_out, bands_out,
    series, column_hi, column_lo, turn, phase, middle, outer_hi, outer_lo, twist, inner_hi, inner_lo, join,
    order, edge, mirror,
    send_one, recv_one, send_two, bins, halo_out, halo_in, rows, mixed, bands,
    load_sem, own_sem, send_sem, recv_sem, halo_send_sem, halo_recv_sem, out_sem, ready,
):
    me = lax.axis_index("grp") * MEMBERS + lax.axis_index("dev")
    pairs = [
        (phase_in.at[me], phase), (series_in, series),
        (column_hi_in.at[0], column_hi.at[0]), (column_lo_in.at[0], column_lo.at[0]), (turn_in, turn),
        (column_hi_in.at[1], column_hi.at[1]), (column_lo_in.at[1], column_lo.at[1]), (middle_in, middle), (outer_hi_in, outer_hi), (outer_lo_in, outer_lo),
        (twist_in, twist), (inner_hi_in, inner_hi), (inner_lo_in, inner_lo), (join_in, join),
        (order_in, order), (edge_in, edge), (mirror_in, mirror),
    ]
    loads = [pltpu.make_async_copy(a, b, load_sem.at[i]) for i, (a, b) in enumerate(pairs)]
    def tell(semaphore, size, target):
        def one(step, carry):
            pl.semaphore_signal(semaphore, inc=1, device_id=target(step), device_id_type=MESH)
            return carry

        lax.fori_loop(1, size, one, 0)

    for load in loads[:5]:
        load.start()
    barrier = pltpu.get_barrier_semaphore()
    group, member = lax.axis_index("grp"), lax.axis_index("dev")
    tell(barrier, GROUPS, lambda step: (lax.rem(group + step, GROUPS), member))
    tell(barrier, MEMBERS, lambda step: (group, lax.rem(member + step, MEMBERS)))
    pl.semaphore_wait(barrier, GROUPS + MEMBERS - 2)
    tell(ready, MEMBERS, lambda step: (group, lax.rem(member + step, MEMBERS)))
    for load in loads[5:]:
        load.start()
    for load in loads[:5]:
        load.wait()

    high, low = split(jnp.concatenate([series[0], series[1]], axis=1))
    padded = jnp.concatenate([phase[...]] * 16, axis=0)
    phase_columns = jnp.transpose(padded)

    def column_part(chunk):
        def rows(part):
            at = pl.ds(part * HALF, HALF)
            return product((column_hi[chunk, at, :], column_lo[chunk, at, :]), (high, low))

        real, imag = rows(0), rows(1)
        blocks = (2 * chunk, 2 * chunk + 1)
        phase_real = jnp.concatenate([phase_columns[:, b : b + 1] for b in blocks], axis=0)
        phase_imag = jnp.concatenate([phase_columns[:, b + 4 : b + 5] for b in blocks], axis=0)
        for e in range(2):
            turn_real = turn[e, 0, pl.ds(chunk * HALF, HALF), :]
            turn_imag = turn[e, 1, pl.ds(chunk * HALF, HALF), :]
            full_real = turn_real * phase_real - turn_imag * phase_imag
            full_imag = turn_real * phase_imag + turn_imag * phase_real
            a, b = real[:, e * LANES : (e + 1) * LANES], imag[:, e * LANES : (e + 1) * LANES]
            send_one[chunk, pl.ds(2 * e, HALF, stride=4), :] = a * full_real - b * full_imag
            send_one[chunk, pl.ds(2 * e + 1, HALF, stride=4), :] = a * full_imag + b * full_real

    def send_all(source, target_ref, chunk, number):
        mine = pl.ds(pl.multiple_of(4 * me, 4), 4)
        own = pltpu.make_async_copy(source.at[chunk, mine], target_ref.at[chunk, mine], own_sem.at[number])
        own.start()

        def send(step, carry):
            target = lax.rem(me + step, DEVICES)
            pltpu.make_async_remote_copy(
                src_ref=source.at[chunk, pl.ds(pl.multiple_of(4 * target, 4), 4)],
                dst_ref=target_ref.at[chunk, mine],
                send_sem=send_sem.at[number],
                recv_sem=recv_sem.at[number],
                device_id=place(target),
                device_id_type=MESH,
            ).start()
            return carry

        lax.fori_loop(1, DEVICES, send, 0, unroll=5)
        own.wait()

    def wait_all(source, target_ref, chunk, sem):
        others = pl.ds(0, 4 * (DEVICES - 1))
        pltpu.make_async_copy(source.at[chunk, others], target_ref.at[chunk, others], sem).wait()

    column_part(0)
    pl.semaphore_wait(ready, MEMBERS - 1)
    send_all(send_one, recv_one, 0, 0)
    for load in loads[5:]:
        load.wait()
    column_part(1)
    send_all(send_one, recv_one, 1, 1)

    def row_part(real, imag):
        wide = product((outer_hi[...], outer_lo[...]), split(jnp.concatenate([real, imag], axis=0)))
        done = []
        for e in range(2):
            a, b = wide[:HALF, e * LANES : (e + 1) * LANES], wide[HALF:, e * LANES : (e + 1) * LANES]
            turned = [a * twist[0] - b * twist[1], a * twist[1] + b * twist[0]]
            done.append(
                product_t((inner_hi[...], inner_lo[...]), split(jnp.concatenate(turned, axis=1)))
            )
        return done

    def store(chunk, part, value, flip):
        for h in range(2):
            first = 4 * (1 - h if flip else h) + part
            send_two[chunk, pl.ds(first, LANES, stride=8), :] = value[:, h * LANES : (h + 1) * LANES]

    def store_direct(chunk, even, odd):
        odd_real, odd_imag = odd[0:128], odd[128:256]
        store(chunk, 0, even[0:128] + (join[0] * odd_real - join[1] * odd_imag), False)
        store(chunk, 1, even[128:256] + (join[0] * odd_imag + join[1] * odd_real), False)

    def store_mirrored(chunk, even, odd):
        odd_real, odd_imag = odd[256:384], odd[384:512]
        store(chunk, 2, even[256:384] - (join[2] * odd_real - join[3] * odd_imag), True)
        store(chunk, 3, (join[2] * odd_imag + join[3] * odd_real) - even[384:512], True)

    def arrived(chunk):
        return [recv_one[chunk, pl.ds(s, HALF, stride=4), :] for s in range(4)]

    def rows_of(chunk):
        parts = arrived(chunk)
        real = jnp.concatenate([parts[0], parts[2]], axis=1)
        imag = jnp.concatenate([parts[1], parts[3]], axis=1)
        if chunk == 0:
            imag = imag * (me != 0).astype(F32)
        even, odd = row_part(real, imag)
        store_direct(chunk, even, odd)
        store_mirrored(chunk, even, odd)

    wait_all(send_one, recv_one, 0, recv_sem.at[0])
    rows_of(0)

    @pl.when(me == 0)
    def _():
        parts = arrived(0)
        real = jnp.concatenate([parts[1] * middle[0, 0], parts[3] * middle[1, 0]], axis=1)
        imag = jnp.concatenate([parts[1] * middle[0, 1], parts[3] * middle[1, 1]], axis=1)
        even, odd = row_part(real, imag)
        store_mirrored(0, even, odd)

    send_all(send_two, bins, 0, 2)
    wait_all(send_one, recv_one, 1, recv_sem.at[1])
    rows_of(1)
    send_all(send_two, bins, 1, 3)

    lane = lax.broadcasted_iota(jnp.int32, (1, LANES), 1)
    for d in range(DRIFTS):
        taps = templates[pl.ds(chosen[d], 1), :]
        tap = lax.rem(lane, TAPS)
        inside = (tap >= TAPS // 2 - reach[d]) & (tap < TAPS // 2 + reach[d])
        taps = jnp.where(inside, taps, 0.0)
        real = jnp.where(lane < TAPS, taps, 0.0)
        imag = jnp.where(lane < TAPS, pltpu.roll(taps, TAPS, 1), 0.0)
        band_real = pltpu.roll(jnp.broadcast_to(real, (TAPS, LANES)), 0, 1, stride=1, stride_axis=0)
        band_imag = pltpu.roll(jnp.broadcast_to(imag, (TAPS, LANES)), 0, 1, stride=1, stride_axis=0)
        for part, wide in enumerate(([band_real, -band_imag], [band_imag, band_real])):
            for level, value in enumerate(split(jnp.concatenate(wide, axis=1))):
                bands[d // 2, level, pl.ds(part * LANES + d % 2 * TAPS, TAPS), :] = value

    bands_copy = pltpu.make_async_copy(bands, bands_out, out_sem.at[0])
    bands_copy.start()

    wait_all(send_two, bins, 0, recv_sem.at[2])

    def halo_rows(side):
        first = (4 + 2, 0)[side]
        return jnp.concatenate([bins[0, pl.ds(first + part, 32, stride=4), :] for part in range(2)], axis=0)

    last = DEVICES - 1
    near = [lax.rem(me + 1, DEVICES), lax.rem(me + last, DEVICES)]
    sends = [me < last, me > 0]
    gets = [me > 0, me < last]
    copies = []
    for side in range(2):
        halo_out[side] = halo_rows(side)
        halo_in[side] = jnp.zeros((64, LANES), F32)
    for side in range(2):
        copy = pltpu.make_async_remote_copy(
            src_ref=halo_out.at[side],
            dst_ref=halo_in.at[2 + side],
            send_sem=halo_send_sem.at[side],
            recv_sem=halo_recv_sem.at[side],
            device_id=place(near[side]),
            device_id_type=MESH,
        )
        pl.when(sends[side])(copy.start)
        copies.append(copy)

    def flip(value):
        return jnp.dot(value.astype(BF16), mirror[...], preferred_element_type=F32).astype(BF16)

    def put_direct(chunk):
        for part in range(2):
            for level, value in enumerate(split(bins[chunk, pl.ds(part, HALF, stride=4), :])):
                rows[2 * level + part, pl.ds(32 + HALF * chunk, HALF), :] = value
            wide = jnp.concatenate(split(bins[chunk, pl.ds(2 + part, HALF, stride=4), :]), axis=1)
            mixed[pl.ds(HALF * chunk, HALF), pl.ds(2 * LANES * part, 2 * LANES)] = wide

    def put_mirrored(moved, first, count):
        for part in range(2):
            for level in range(2):
                at = (2 * part + level) * LANES
                rows[2 * level + part, pl.ds(first, count), :] = flip(moved[:, at : at + LANES])

    put_direct(0)
    moved = jnp.dot(order[pl.ds(HALF, HALF), pl.ds(0, HALF)], mixed[pl.ds(0, HALF), :], preferred_element_type=F32)
    put_mirrored(moved, 800, HALF)

    first_lane = lax.broadcasted_iota(jnp.int32, (64, LANES), 1) == 0
    sides = []
    for side in range(2):
        pl.when(gets[side])(copies[side].wait_recv)

        @pl.when(gets[side])
        def _():
            halo_in[side] = halo_in[2 + side]

        sides.append(split(pltpu.roll(jnp.where(first_lane, halo_in[side], halo_out[side]), LANES - 1, 1)))
        pl.when(sends[side])(copies[side].wait_send)
    moved = jnp.dot(edge[...], jnp.concatenate(sides[0], axis=1), preferred_element_type=F32)
    for level in range(2):
        flipped = flip(moved[:, level * LANES : (level + 1) * LANES])
        for part in range(2):
            rows[2 * level + part, pl.ds(0, 32), :] = flipped[32 * part : 32 * part + 32]
            rows[2 * level + part, pl.ds(1056, 32), :] = sides[1][level][32 * part : 32 * part + 32]

    def rows_part(number, first, count):
        at = pl.ds(first, count)
        copy = pltpu.make_async_copy(rows.at[:, at], rows_out.at[:, at], out_sem.at[number])
        copy.start()
        return copy

    rows_copies = [rows_part(1, 0, 288), rows_part(2, 816, 272)]
    wait_all(send_two, bins, 1, recv_sem.at[3])
    put_direct(1)
    moved = jnp.dot(order[pl.ds(0, 272), :], mixed[...], preferred_element_type=F32)
    put_mirrored(moved, 544, 272)
    rows_copies.append(rows_part(3, 288, 528))
    for number, source, target_ref in (
        (0, send_one, recv_one), (1, send_one, recv_one), (2, send_two, bins), (3, send_two, bins)
    ):
        wait_all(source, target_ref, number % 2, send_sem.at[number])
    for copy in (bands_copy, *rows_copies):
        copy.wait()


def correlate_kernel(rows_in, bands_in, out, rows, bands, *rest):
    tiles, (row_sem, band_sem, out_sem) = rest[:8], rest[8:]
    row_copy = pltpu.make_async_copy(rows_in, rows, row_sem)
    row_copy.start()
    band_copies = []
    for pair in range(DRIFTS // 2):
        copy = pltpu.make_async_copy(bands_in.at[pair], bands.at[pair], band_sem.at[pair])
        copy.start()
        band_copies.append(copy)

    def windows_of(tile):
        def window(level, odd):
            at = pl.ds(tile * LANES + odd * TAPS, LANES)
            return jnp.concatenate([jnp.transpose(rows[2 * level + part, at, :]) for part in range(2)], axis=1)

        return [jnp.concatenate([window(level, odd) for odd in range(2)], axis=0) for level in range(2)]

    low_lanes = lax.broadcasted_iota(jnp.int32, (LANES, LANES), 1) < TAPS
    copies = []
    row_copy.wait()
    for copy in band_copies:
        copy.wait()
    coming, following = windows_of(0), windows_of(1)
    for half in range(4):
        both = (2 * half, 2 * half + 1)
        windows = [jnp.concatenate([first, second], axis=0) for first, second in zip(coming, following)]
        if half < 3:
            coming, following = windows_of(2 * half + 2), windows_of(2 * half + 3)
        for pair in range(DRIFTS // 2):
            response = product_t(windows, (bands[pair, 0], bands[pair, 1]))
            real, imag = response[:, :LANES], response[:, LANES:]
            power = real * real + imag * imag
            for tile in both:
                flat = tiles[tile].reshape(2 * LANES * 8, LANES)
                at = 2 * LANES * (tile % 2)
                even, odd = power[at : at + LANES], power[at + LANES : at + 2 * LANES]
                first = jnp.where(low_lanes, even, pltpu.roll(odd, TAPS, 1))
                second = jnp.where(low_lanes, pltpu.roll(even, TAPS, 1), odd)
                for d, value in ((2 * pair, first), (2 * pair + 1, second)):
                    flat[pl.ds(d // 8 * LANES * 8 + d % 8, LANES, stride=8), :] = value
            if pair % 4 == 3:
                for tile in both:
                    block = pair // 4
                    copy = pltpu.make_async_copy(
                        tiles[tile].at[block], out.at[block, :, tile], out_sem.at[2 * tile + block]
                    )
                    copy.start()
                    copies.append(copy)
    for copy in copies:
        copy.wait()


def spectrum(series, templates, drift_template, drift_reach):
    made = tables()
    inputs = [
        series, *made["column"], made["turn"], made["phase"], made["middle"], *made["outer"],
        made["twist"], *made["inner"], made["join"], made["order"], made["edge"], made["mirror"],
    ]
    inputs = [jnp.asarray(value) for value in inputs]
    shapes = [value.shape for value in inputs]
    shapes[4] = (8, LANES)
    copies = [pltpu.VMEM(shape, value.dtype) for shape, value in zip(shapes, inputs)]
    chunked = pltpu.VMEM((2, 4 * DEVICES, LANES), F32)
    far = pl.BlockSpec(memory_space=pl.ANY)
    smem = pl.BlockSpec(memory_space=pltpu.SMEM)
    dma = pltpu.SemaphoreType.DMA
    bands = (DRIFTS // 2, 2, 256, 256)
    return pl.pallas_call(
        spectrum_kernel,
        name="spectrum",
        out_shape=(
            jax.ShapeDtypeStruct((4, EXTENDED, LANES), BF16),
            jax.ShapeDtypeStruct(bands, BF16),
        ),
        in_specs=[far] * len(inputs) + [pl.BlockSpec(memory_space=pltpu.VMEM), smem, smem],
        out_specs=(far, far),
        scratch_shapes=[
            *copies, chunked, chunked, chunked, chunked,
            pltpu.VMEM((2, 64, LANES), F32), pltpu.VMEM((4, 64, LANES), F32),
            pltpu.VMEM((4, EXTENDED, LANES), BF16), pltpu.VMEM((512, 512), BF16),
            pltpu.VMEM(bands, BF16),
            dma((len(inputs) + 2,)), dma((4,)), dma((4,)), dma((4,)), dma((2,)), dma((2,)), dma((4,)),
            pltpu.SemaphoreType.REGULAR,
        ],
        compiler_params=pltpu.CompilerParams(
            collective_id=0, has_side_effects=True, vmem_limit_bytes=60 << 20
        ),
    )(*inputs, templates, drift_template, drift_reach)


def correlate(rows, bands):
    far = pl.BlockSpec(memory_space=pl.ANY)
    dma = pltpu.SemaphoreType.DMA
    powers = pl.pallas_call(
        correlate_kernel,
        name="correlate",
        out_shape=jax.ShapeDtypeStruct((2, LANES, 8, 8, LANES), F32),
        in_specs=[far] * 2,
        out_specs=far,
        scratch_shapes=[
            pltpu.VMEM(rows.shape, BF16), pltpu.VMEM(bands.shape, BF16),
            *[pltpu.VMEM((2, LANES, 8, LANES), F32) for _ in range(8)],
            dma, dma((DRIFTS // 2,)), dma((16,)),
        ],
        compiler_params=pltpu.CompilerParams(vmem_limit_bytes=60 << 20),
    )(rows, bands)
    return powers.transpose(0, 3, 1, 2, 4).reshape(DRIFTS, LANES * ROWS)


def local(series, templates, drift_template, drift_reach):
    return correlate(*spectrum(series, templates, drift_template, drift_reach))


def solution(mesh):
    return jax.shard_map(
        local,
        mesh=mesh,
        in_specs=(P(None, None, ("grp", "dev")), P(), P(), P()),
        out_specs=P(None, ("grp", "dev")),
        check_vma=False,
    )
```

```python
import functools
import math

import jax
import jax.numpy as jnp
import ml_dtypes
import numpy as np
from jax import lax
from jax.experimental import pallas as pl
from jax.experimental.pallas import tpu as pltpu
from jax.sharding import PartitionSpec as P

N = 67108864
ROWS = 1024
HALF = 256
LANES = 128
TAPS = 64
DRIFTS = 16
DEVICES = 256
MEMBERS = 32
GROUPS = 8
EXTENDED = 1088
F32 = jnp.float32
BF16 = jnp.bfloat16
MESH = pl.DeviceIdType.MESH


def root(product, length):
    angles = (np.asarray(product, np.int64) % length) * (-2.0 * math.pi / length)
    return np.cos(angles), np.sin(angles)


def halves(table):
    table = np.asarray(table, np.float32)
    high = table.astype(ml_dtypes.bfloat16)
    low = (table - high.astype(np.float32)).astype(ml_dtypes.bfloat16)
    return high, low


@functools.cache
def tables():
    index = np.arange
    done = {}
    cos, sin = root(index(512)[:, None] * index(ROWS)[None, :], ROWS)
    sin[0] = 1.0 - 2.0 * (index(ROWS) % 2)
    column = np.stack([cos, sin]).reshape(2, 2, HALF, ROWS).transpose(1, 0, 2, 3)
    done["column"] = halves(column.reshape(2, 512, ROWS))
    sample = 2 * index(LANES)[None, :] + index(2)[:, None]
    turn = root(sample[:, None, :] * index(512)[None, :, None], N)
    done["turn"] = (np.stack(turn, axis=1) / math.sqrt(N)).astype(np.float32)
    phase = root(2 * LANES * index(DEVICES)[:, None] * index(512)[None, :], N)
    done["phase"] = np.stack(phase, axis=1).reshape(DEVICES, 8, LANES).astype(np.float32)
    middle = root(512 * (2 * LANES * index(HALF)[None, :, None] + sample[:, None, :]), N)
    done["middle"] = np.stack(middle, axis=1).astype(np.float32)
    cos, sin = root(index(HALF)[:, None] * index(HALF)[None, :], HALF)
    done["outer"] = halves(np.block([[cos, -sin], [sin, cos]]))
    twist = root(index(HALF)[:, None] * index(LANES)[None, :], HALF * LANES)
    done["twist"] = np.stack(twist).astype(np.float32)
    cos, sin = root(index(LANES)[:, None] * index(LANES)[None, :], LANES)
    back = slice(None, None, -1)
    done["inner"] = halves(np.block([[cos, -sin], [sin, cos], [cos[back], -sin[back]], [sin[back], cos[back]]]))
    join = np.stack(root(index(HALF)[None, :] + HALF * index(LANES)[:, None], 2 * HALF * LANES))
    done["join"] = np.concatenate([join, join[:, back]]).astype(np.float32)
    order = np.zeros((512, 512), np.float32)
    for row in range(512):
        source = 512 - row
        order[row, source if row else 0] = 1.0
    done["order"] = order.astype(ml_dtypes.bfloat16)
    edge = np.zeros((64, 64), np.float32)
    for row in range(64):
        edge[row, row // 32 * 32 + 31 - row % 32] = 1.0
    done["edge"] = edge.astype(ml_dtypes.bfloat16)
    done["mirror"] = np.eye(LANES, dtype=np.float32)[back].astype(ml_dtypes.bfloat16)
    return done


def split(value):
    high = value.astype(BF16)
    return high, (value - high.astype(F32)).astype(BF16)


def product(left, right):
    dot = functools.partial(jnp.dot, preferred_element_type=F32)
    return dot(left[0], right[0]) + (dot(left[0], right[1]) + dot(left[1], right[0]))


def product_t(left, right):
    def dot(a, b):
        return lax.dot_general(a, b, (((1,), (1,)), ((), ())), preferred_element_type=F32)

    return dot(left[0], right[0]) + (dot(left[0], right[1]) + dot(left[1], right[0]))


def place(target):
    return (target // MEMBERS, lax.rem(target, MEMBERS))


def spectrum_kernel(
    series_in, column_hi_in, column_lo_in, turn_in, phase_in, middle_in, outer_hi_in, outer_lo_in,
    twist_in, inner_hi_in, inner_lo_in, join_in, order_in, edge_in, mirror_in, templates, chosen, reach,
    rows_out, bands_out,
    series, column_hi, column_lo, turn, phase, middle, outer_hi, outer_lo, twist, inner_hi, inner_lo, join,
    order, edge, mirror,
    send_one, recv_one, send_two, bins, halo_out, halo_in, rows, mixed, bands,
    load_sem, own_sem, send_sem, recv_sem, halo_send_sem, halo_recv_sem, out_sem, ready,
):
    me = lax.axis_index("grp") * MEMBERS + lax.axis_index("dev")
    pairs = [
        (phase_in.at[me], phase), (series_in, series),
        (column_hi_in.at[0], column_hi.at[0]), (column_lo_in.at[0], column_lo.at[0]), (turn_in, turn),
        (column_hi_in.at[1], column_hi.at[1]), (column_lo_in.at[1], column_lo.at[1]), (middle_in, middle), (outer_hi_in, outer_hi), (outer_lo_in, outer_lo),
        (twist_in, twist), (inner_hi_in, inner_hi), (inner_lo_in, inner_lo), (join_in, join),
        (order_in, order), (edge_in, edge), (mirror_in, mirror),
    ]
    loads = [pltpu.make_async_copy(a, b, load_sem.at[i]) for i, (a, b) in enumerate(pairs)]
    def tell(semaphore, size, target):
        def one(step, carry):
            pl.semaphore_signal(semaphore, inc=1, device_id=target(step), device_id_type=MESH)
            return carry

        lax.fori_loop(1, size, one, 0)

    for load in loads[:5]:
        load.start()
    barrier = pltpu.get_barrier_semaphore()
    group, member = lax.axis_index("grp"), lax.axis_index("dev")
    tell(barrier, GROUPS, lambda step: (lax.rem(group + step, GROUPS), member))
    tell(barrier, MEMBERS, lambda step: (group, lax.rem(member + step, MEMBERS)))
    pl.semaphore_wait(barrier, GROUPS + MEMBERS - 2)
    tell(ready, MEMBERS, lambda step: (group, lax.rem(member + step, MEMBERS)))
    for load in loads[5:]:
        load.start()
    for load in loads[:5]:
        load.wait()

    high, low = split(jnp.concatenate([series[0], series[1]], axis=1))
    padded = jnp.concatenate([phase[...]] * 16, axis=0)
    phase_columns = jnp.transpose(padded)

    def column_part(chunk):
        def rows(part):
            at = pl.ds(part * HALF, HALF)
            return product((column_hi[chunk, at, :], column_lo[chunk, at, :]), (high, low))

        real, imag = rows(0), rows(1)
        blocks = (2 * chunk, 2 * chunk + 1)
        phase_real = jnp.concatenate([phase_columns[:, b : b + 1] for b in blocks], axis=0)
        phase_imag = jnp.concatenate([phase_columns[:, b + 4 : b + 5] for b in blocks], axis=0)
        for e in range(2):
            turn_real = turn[e, 0, pl.ds(chunk * HALF, HALF), :]
            turn_imag = turn[e, 1, pl.ds(chunk * HALF, HALF), :]
            full_real = turn_real * phase_real - turn_imag * phase_imag
            full_imag = turn_real * phase_imag + turn_imag * phase_real
            a, b = real[:, e * LANES : (e + 1) * LANES], imag[:, e * LANES : (e + 1) * LANES]
            send_one[chunk, pl.ds(2 * e, HALF, stride=4), :] = a * full_real - b * full_imag
            send_one[chunk, pl.ds(2 * e + 1, HALF, stride=4), :] = a * full_imag + b * full_real

    def send_all(source, target_ref, chunk, number):
        mine = pl.ds(pl.multiple_of(4 * me, 4), 4)
        own = pltpu.make_async_copy(source.at[chunk, mine], target_ref.at[chunk, mine], own_sem.at[number])
        own.start()

        def send(step, carry):
            target = lax.rem(me + step, DEVICES)
            pltpu.make_async_remote_copy(
                src_ref=source.at[chunk, pl.ds(pl.multiple_of(4 * target, 4), 4)],
                dst_ref=target_ref.at[chunk, mine],
                send_sem=send_sem.at[number],
                recv_sem=recv_sem.at[number],
                device_id=place(target),
                device_id_type=MESH,
            ).start()
            return carry

        lax.fori_loop(1, DEVICES, send, 0, unroll=5)
        own.wait()

    def wait_all(source, target_ref, chunk, sem):
        others = pl.ds(0, 4 * (DEVICES - 1))
        pltpu.make_async_copy(source.at[chunk, others], target_ref.at[chunk, others], sem).wait()

    column_part(0)
    pl.semaphore_wait(ready, MEMBERS - 1)
    send_all(send_one, recv_one, 0, 0)
    for load in loads[5:]:
        load.wait()
    column_part(1)
    send_all(send_one, recv_one, 1, 1)

    def row_part(real, imag):
        wide = product((outer_hi[...], outer_lo[...]), split(jnp.concatenate([real, imag], axis=0)))
        done = []
        for e in range(2):
            a, b = wide[:HALF, e * LANES : (e + 1) * LANES], wide[HALF:, e * LANES : (e + 1) * LANES]
            turned = [a * twist[0] - b * twist[1], a * twist[1] + b * twist[0]]
            done.append(
                product_t((inner_hi[...], inner_lo[...]), split(jnp.concatenate(turned, axis=1)))
            )
        return done

    def store(chunk, part, value, flip):
        for h in range(2):
            first = 4 * (1 - h if flip else h) + part
            send_two[chunk, pl.ds(first, LANES, stride=8), :] = value[:, h * LANES : (h + 1) * LANES]

    def store_direct(chunk, even, odd):
        odd_real, odd_imag = odd[0:128], odd[128:256]
        store(chunk, 0, even[0:128] + (join[0] * odd_real - join[1] * odd_imag), False)
        store(chunk, 1, even[128:256] + (join[0] * odd_imag + join[1] * odd_real), False)

    def store_mirrored(chunk, even, odd):
        odd_real, odd_imag = odd[256:384], odd[384:512]
        store(chunk, 2, even[256:384] - (join[2] * odd_real - join[3] * odd_imag), True)
        store(chunk, 3, (join[2] * odd_imag + join[3] * odd_real) - even[384:512], True)

    def arrived(chunk):
        return [recv_one[chunk, pl.ds(s, HALF, stride=4), :] for s in range(4)]

    def rows_of(chunk):
        parts = arrived(chunk)
        real = jnp.concatenate([parts[0], parts[2]], axis=1)
        imag = jnp.concatenate([parts[1], parts[3]], axis=1)
        if chunk == 0:
            imag = imag * (me != 0).astype(F32)
        even, odd = row_part(real, imag)
        store_direct(chunk, even, odd)
        store_mirrored(chunk, even, odd)

    wait_all(send_one, recv_one, 0, recv_sem.at[0])
    rows_of(0)

    @pl.when(me == 0)
    def _():
        parts = arrived(0)
        real = jnp.concatenate([parts[1] * middle[0, 0], parts[3] * middle[1, 0]], axis=1)
        imag = jnp.concatenate([parts[1] * middle[0, 1], parts[3] * middle[1, 1]], axis=1)
        even, odd = row_part(real, imag)
        store_mirrored(0, even, odd)

    send_all(send_two, bins, 0, 2)
    wait_all(send_one, recv_one, 1, recv_sem.at[1])
    rows_of(1)
    send_all(send_two, bins, 1, 3)

    lane = lax.broadcasted_iota(jnp.int32, (1, LANES), 1)
    for d in range(DRIFTS):
        taps = templates[pl.ds(chosen[d], 1), :]
        tap = lax.rem(lane, TAPS)
        inside = (tap >= TAPS // 2 - reach[d]) & (tap < TAPS // 2 + reach[d])
        taps = jnp.where(inside, taps, 0.0)
        real = jnp.where(lane < TAPS, taps, 0.0)
        imag = jnp.where(lane < TAPS, pltpu.roll(taps, TAPS, 1), 0.0)
        band_real = pltpu.roll(jnp.broadcast_to(real, (TAPS, LANES)), 0, 1, stride=1, stride_axis=0)
        band_imag = pltpu.roll(jnp.broadcast_to(imag, (TAPS, LANES)), 0, 1, stride=1, stride_axis=0)
        for part, wide in enumerate(([band_real, -band_imag], [band_imag, band_real])):
            for level, value in enumerate(split(jnp.concatenate(wide, axis=1))):
                bands[d // 2, level, pl.ds(part * LANES + d % 2 * TAPS, TAPS), :] = value

    bands_copy = pltpu.make_async_copy(bands, bands_out, out_sem.at[0])
    bands_copy.start()

    wait_all(send_two, bins, 0, recv_sem.at[2])

    def halo_rows(side):
        first = (4 + 2, 0)[side]
        return jnp.concatenate([bins[0, pl.ds(first + part, 32, stride=4), :] for part in range(2)], axis=0)

    last = DEVICES - 1
    near = [lax.rem(me + 1, DEVICES), lax.rem(me + last, DEVICES)]
    sends = [me < last, me > 0]
    gets = [me > 0, me < last]
    copies = []
    for side in range(2):
        halo_out[side] = halo_rows(side)
        halo_in[side] = jnp.zeros((64, LANES), F32)
    for side in range(2):
        copy = pltpu.make_async_remote_copy(
            src_ref=halo_out.at[side],
            dst_ref=halo_in.at[2 + side],
            send_sem=halo_send_sem.at[side],
            recv_sem=halo_recv_sem.at[side],
            device_id=place(near[side]),
            device_id_type=MESH,
        )
        pl.when(sends[side])(copy.start)
        copies.append(copy)

    def flip(value):
        return jnp.dot(value.astype(BF16), mirror[...], preferred_element_type=F32).astype(BF16)

    def put_direct(chunk):
        for part in range(2):
            for level, value in enumerate(split(bins[chunk, pl.ds(part, HALF, stride=4), :])):
                rows[2 * level + part, pl.ds(32 + HALF * chunk, HALF), :] = value
            wide = jnp.concatenate(split(bins[chunk, pl.ds(2 + part, HALF, stride=4), :]), axis=1)
            mixed[pl.ds(HALF * chunk, HALF), pl.ds(2 * LANES * part, 2 * LANES)] = wide

    def put_mirrored(moved, first, count):
        for part in range(2):
            for level in range(2):
                at = (2 * part + level) * LANES
                rows[2 * level + part, pl.ds(first, count), :] = flip(moved[:, at : at + LANES])

    put_direct(0)
    moved = jnp.dot(order[pl.ds(HALF, HALF), pl.ds(0, HALF)], mixed[pl.ds(0, HALF), :], preferred_element_type=F32)
    put_mirrored(moved, 800, HALF)

    first_lane = lax.broadcasted_iota(jnp.int32, (64, LANES), 1) == 0
    sides = []
    for side in range(2):
        pl.when(gets[side])(copies[side].wait_recv)

        @pl.when(gets[side])
        def _():
            halo_in[side] = halo_in[2 + side]

        sides.append(split(pltpu.roll(jnp.where(first_lane, halo_in[side], halo_out[side]), LANES - 1, 1)))
        pl.when(sends[side])(copies[side].wait_send)
    moved = jnp.dot(edge[...], jnp.concatenate(sides[0], axis=1), preferred_element_type=F32)
    for level in range(2):
        flipped = flip(moved[:, level * LANES : (level + 1) * LANES])
        for part in range(2):
            rows[2 * level + part, pl.ds(0, 32), :] = flipped[32 * part : 32 * part + 32]
            rows[2 * level + part, pl.ds(1056, 32), :] = sides[1][level][32 * part : 32 * part + 32]

    def rows_part(number, first, count):
        at = pl.ds(first, count)
        copy = pltpu.make_async_copy(rows.at[:, at], rows_out.at[:, at], out_sem.at[number])
        copy.start()
        return copy

    rows_copies = [rows_part(1, 0, 288), rows_part(2, 816, 272)]
    wait_all(send_two, bins, 1, recv_sem.at[3])
    put_direct(1)
    moved = jnp.dot(order[pl.ds(0, 272), :], mixed[...], preferred_element_type=F32)
    put_mirrored(moved, 544, 272)
    rows_copies.append(rows_part(3, 288, 528))
    for number, source, target_ref in (
        (0, send_one, recv_one), (1, send_one, recv_one), (2, send_two, bins), (3, send_two, bins)
    ):
        wait_all(source, target_ref, number % 2, send_sem.at[number])
    for copy in (bands_copy, *rows_copies):
        copy.wait()


def correlate_kernel(rows_in, bands_in, out, rows, bands, *rest):
    tiles, (row_sem, band_sem, out_sem) = rest[:8], rest[8:]
    row_copy = pltpu.make_async_copy(rows_in, rows, row_sem)
    row_copy.start()
    band_copies = []
    for pair in range(DRIFTS // 2):
        copy = pltpu.make_async_copy(bands_in.at[pair], bands.at[pair], band_sem.at[pair])
        copy.start()
        band_copies.append(copy)

    def windows_of(tile):
        def window(level, odd):
            at = pl.ds(tile * LANES + odd * TAPS, LANES)
            return jnp.concatenate([jnp.transpose(rows[2 * level + part, at, :]) for part in range(2)], axis=1)

        return [jnp.concatenate([window(level, odd) for odd in range(2)], axis=0) for level in range(2)]

    low_lanes = lax.broadcasted_iota(jnp.int32, (LANES, LANES), 1) < TAPS
    copies = []
    row_copy.wait()
    coming, following = windows_of(0), windows_of(1)
    for copy in band_copies:
        copy.wait()
    for half in range(4):
        both = (2 * half, 2 * half + 1)
        windows = [jnp.concatenate([first, second], axis=0) for first, second in zip(coming, following)]
        if half < 3:
            coming, following = windows_of(2 * half + 2), windows_of(2 * half + 3)
        for pair in range(DRIFTS // 2):
            response = product_t(windows, (bands[pair, 0], bands[pair, 1]))
            real, imag = response[:, :LANES], response[:, LANES:]
            power = real * real + imag * imag
            for tile in both:
                flat = tiles[tile].reshape(2 * LANES * 8, LANES)
                at = 2 * LANES * (tile % 2)
                even, odd = power[at : at + LANES], power[at + LANES : at + 2 * LANES]
                first = jnp.where(low_lanes, even, pltpu.roll(odd, TAPS, 1))
                second = jnp.where(low_lanes, pltpu.roll(even, TAPS, 1), odd)
                for d, value in ((2 * pair, first), (2 * pair + 1, second)):
                    flat[pl.ds(d // 8 * LANES * 8 + d % 8, LANES, stride=8), :] = value
            if pair % 4 == 3:
                for tile in both:
                    block = pair // 4
                    copy = pltpu.make_async_copy(
                        tiles[tile].at[block], out.at[block, :, tile], out_sem.at[2 * tile + block]
                    )
                    copy.start()
                    copies.append(copy)
    for copy in copies:
        copy.wait()


def spectrum(series, templates, drift_template, drift_reach):
    made = tables()
    inputs = [
        series, *made["column"], made["turn"], made["phase"], made["middle"], *made["outer"],
        made["twist"], *made["inner"], made["join"], made["order"], made["edge"], made["mirror"],
    ]
    inputs = [jnp.asarray(value) for value in inputs]
    shapes = [value.shape for value in inputs]
    shapes[4] = (8, LANES)
    copies = [pltpu.VMEM(shape, value.dtype) for shape, value in zip(shapes, inputs)]
    chunked = pltpu.VMEM((2, 4 * DEVICES, LANES), F32)
    far = pl.BlockSpec(memory_space=pl.ANY)
    smem = pl.BlockSpec(memory_space=pltpu.SMEM)
    dma = pltpu.SemaphoreType.DMA
    bands = (DRIFTS // 2, 2, 256, 256)
    return pl.pallas_call(
        spectrum_kernel,
        name="spectrum",
        out_shape=(
            jax.ShapeDtypeStruct((4, EXTENDED, LANES), BF16),
            jax.ShapeDtypeStruct(bands, BF16),
        ),
        in_specs=[far] * len(inputs) + [pl.BlockSpec(memory_space=pltpu.VMEM), smem, smem],
        out_specs=(far, far),
        scratch_shapes=[
            *copies, chunked, chunked, chunked, chunked,
            pltpu.VMEM((2, 64, LANES), F32), pltpu.VMEM((4, 64, LANES), F32),
            pltpu.VMEM((4, EXTENDED, LANES), BF16), pltpu.VMEM((512, 512), BF16),
            pltpu.VMEM(bands, BF16),
            dma((len(inputs) + 2,)), dma((4,)), dma((4,)), dma((4,)), dma((2,)), dma((2,)), dma((4,)),
            pltpu.SemaphoreType.REGULAR,
        ],
        compiler_params=pltpu.CompilerParams(
            collective_id=0, has_side_effects=True, vmem_limit_bytes=60 << 20
        ),
    )(*inputs, templates, drift_template, drift_reach)


def correlate(rows, bands):
    far = pl.BlockSpec(memory_space=pl.ANY)
    dma = pltpu.SemaphoreType.DMA
    powers = pl.pallas_call(
        correlate_kernel,
        name="correlate",
        out_shape=jax.ShapeDtypeStruct((2, LANES, 8, 8, LANES), F32),
        in_specs=[far] * 2,
        out_specs=far,
        scratch_shapes=[
            pltpu.VMEM(rows.shape, BF16), pltpu.VMEM(bands.shape, BF16),
            *[pltpu.VMEM((2, LANES, 8, LANES), F32) for _ in range(8)],
            dma, dma((DRIFTS // 2,)), dma((16,)),
        ],
        compiler_params=pltpu.CompilerParams(vmem_limit_bytes=60 << 20),
    )(rows, bands)
    return powers.transpose(0, 3, 1, 2, 4).reshape(DRIFTS, LANES * ROWS)


def local(series, templates, drift_template, drift_reach):
    return correlate(*spectrum(series, templates, drift_template, drift_reach))


def solution(mesh):
    return jax.shard_map(
        local,
        mesh=mesh,
        in_specs=(P(None, None, ("grp", "dev")), P(), P(), P()),
        out_specs=P(None, ("grp", "dev")),
        check_vma=False,
    )
```
